128 devices in a mesh: band: 8 (over z, core), grp: 16 (over x, y).
Axes of the slice: x: 4, y: 4, z: 4, core: 2. Of those that a mesh axis runs over, the one named last changes fastest.
Arguments:
- action: float32 [1296, 65536], P(None, ('band', 'grp')), may hold values from 0.05 to 2
- block_list: int32 [512], P(('band', 'grp')), may hold values from 0 to 63, as said below
- land_sea: int32 [32, 2048], P('band', 'grp'), may hold values from 0 to 1, as said below
- ice: int32 [32, 2048], P('band', 'grp'), may hold values 0 or 1
- depth: float32 [32, 2048], P('band', 'grp'), may hold values from 0.2 to 4
- current_x: float32 [32, 2048], P('band', 'grp'), may hold values from -0.15 to 0.15
- current_y: float32 [32, 2048], P('band', 'grp'), may hold values from -0.15 to 0.15
- wind: float32 [32, 2048], P('band', 'grp'), may hold values from 0.3 to 3
- wind_rate: float32 [1296], replicated, may hold values from 0.05 to 0.5
- dissipation: float32 [1296], replicated, may hold values from 0.05 to 0.5
- mix_first: bfloat16 [1296, 1296], replicated, may hold values from -0.15625 to 0.15625
- mix_second: bfloat16 [1296, 1296], replicated, may hold values from -0.15625 to 0.15625
Outputs:
- spectra: float32 [1296, 65536], P(None, ('band', 'grp'))
The draws below stay inside these ranges and needn't reach their ends.
Inputs may be any that keep to these rules, and one draw needn't show every extreme that they name: `block_list`: values are block numbers within a sub-band. The lists of the devices of one sub-band (the entries of one run of 64) name each of its blocks once; in each device's run of 4 entries the first 2 name blocks holding at least one sea cell and the others name blocks of land only. `land_sea`: consistent with block_list: blocks of land only are all 0.
All inputs are finite; a program needn't handle non-finite values. No bound on the sum of `ice` on one device may be relied on, other than what follows from the above.
Results may differ from the reference program's by a relative error of at most 0.0016.
Values may be sent and summed in bfloat16 or wider, within the bound.
A program may use at most 128 MiB of HBM per device.

```python
import math
import jax
import jax.numpy as jnp
from jax import lax

ND = 36
NF = 36
K = 1296
RY = 4
BLK = 128
STEPS = 2
NY = 32
NX = 2048
BLK_DEV = 4
WET_DEV = 2
BAND_BLOCKS = 64
ROW_BLOCKS = 16


def block_layout(key):
    bands = NY // RY
    keys = jax.random.split(key, bands)
    return jax.vmap(lambda one: jax.random.permutation(one, BAND_BLOCKS))(keys).astype(jnp.int32)


def draw_block_list(key, part):
    orders = block_layout(key)
    bands = NY // RY
    members = BAND_BLOCKS // BLK_DEV
    seaward = orders[:, :WET_DEV * members].reshape(bands, members, WET_DEV)
    landward = orders[:, WET_DEV * members:].reshape(bands, members, BLK_DEV - WET_DEV)
    return jnp.concatenate([seaward, landward], axis=2).reshape(-1).astype(jnp.int32)


def draw_land_sea(key, part):
    orders = block_layout(key)
    key = jax.random.fold_in(key, 7)
    bands = NY // RY
    members = BAND_BLOCKS // BLK_DEV
    ranks = jax.vmap(lambda order: jnp.zeros((BAND_BLOCKS,), jnp.int32).at[order].set(jnp.arange(BAND_BLOCKS, dtype=jnp.int32)))(orders)
    sea_block = ranks < WET_DEV * members
    coast = jax.random.randint(jax.random.fold_in(key, 1), (bands, BAND_BLOCKS, BLK), 0, 5) > 0
    anchor = jax.random.randint(jax.random.fold_in(key, 2), (bands, BAND_BLOCKS, 1), 0, BLK)
    sure = jnp.arange(BLK, dtype=jnp.int32)[None, None, :] == anchor
    cells = jnp.logical_and(jnp.logical_or(coast, sure), sea_block[:, :, None])
    return cells.astype(jnp.int32).reshape(bands, RY, ROW_BLOCKS, BLK).reshape(NY, NX)


def touch_ends(entries, own_key, low, high):
    dims = entries.shape
    spot = [jax.random.randint(jax.random.fold_in(own_key, axis), (), 0, dims[axis]) for axis in range(len(dims))]
    entries = entries.at[tuple(spot)].set(low)
    longest = dims.index(max(dims))
    spot[longest] = (spot[longest] + 1) % dims[longest]
    return entries.at[tuple(spot)].set(high)


def shard_levels(rng, shape, cuts, least, top_value):
    level, own = 1.0, jax.random.fold_in(rng, 6)
    for axis_at, parts in cuts:
        heights = jnp.exp(jax.random.uniform(jax.random.fold_in(own, axis_at), (parts,), jnp.float32, least / len(cuts), top_value / len(cuts)))
        level = level * jnp.repeat(heights, shape[axis_at] // parts).reshape([-1 if axis == axis_at else 1 for axis in range(len(shape))])
    return level


def scatter_about(stream_key, extent, deviation, bound, kind=jnp.bfloat16):
    return jnp.clip(deviation * jax.random.normal(stream_key, extent, jnp.float32), -bound, bound).astype(kind)


def setup_inputs(seed: int = 0) -> dict:
    key_of = jax.random.split(jax.random.key(seed), 13)
    action = jnp.clip(jnp.exp(math.log(2.0) - 3.6888794 * jax.random.uniform(key_of[0], (K, NY * NX), jnp.float32) ** shard_levels(key_of[0], (K, NY * NX), ((1, 128),), -0.2, 0.2)), 0.05, 2.0)
    block_list = draw_block_list(jax.random.fold_in(key_of[12], 71), 0)
    land_sea = draw_land_sea(jax.random.fold_in(key_of[12], 71), 0)
    ice = touch_ends((jax.random.randint(key_of[3], (NY, NX), 0, 8) < 1).astype(jnp.int32), jax.random.fold_in(key_of[3], 1), 0, 1)
    depth = jnp.clip(jnp.exp(math.log(4.0) - 2.9957323 * jax.random.uniform(key_of[4], (NY, NX), jnp.float32) ** shard_levels(key_of[4], (NY, NX), ((0, 8), (1, 16)), -0.2, 0.2)), 0.2, 4.0)
    current_x = jnp.clip(jax.random.uniform(key_of[5], (NY, NX), jnp.float32, -0.15, 0.15) * shard_levels(key_of[5], (NY, NX), ((0, 8), (1, 16)), -0.4, 0.0), -0.15, 0.15)
    current_y = jnp.clip(jax.random.uniform(key_of[6], (NY, NX), jnp.float32, -0.15, 0.15) * shard_levels(key_of[6], (NY, NX), ((0, 8), (1, 16)), -0.4, 0.0), -0.15, 0.15)
    wind = jnp.clip(jnp.exp(math.log(3.0) - 2.3025851 * jax.random.uniform(key_of[7], (NY, NX), jnp.float32) ** shard_levels(key_of[7], (NY, NX), ((0, 8), (1, 16)), -0.2, 0.2)), 0.3, 3.0)
    wind_rate = jnp.clip(jnp.exp(jax.random.uniform(key_of[8], (K,), jnp.float32, math.log(0.05), math.log(0.5))), 0.05, 0.5)
    dissipation = jnp.clip(jnp.exp(jax.random.uniform(key_of[9], (K,), jnp.float32, math.log(0.05), math.log(0.5))), 0.05, 0.5)
    mix_first = scatter_about(key_of[10], (K, K), K ** -0.5, 0.15625)
    mix_second = scatter_about(key_of[11], (K, K), K ** -0.5, 0.15625)
    return {"action": action, "block_list": block_list, "land_sea": land_sea, "ice": ice, "depth": depth, "current_x": current_x, "current_y": current_y, "wind": wind, "wind_rate": wind_rate, "dissipation": dissipation, "mix_first": mix_first, "mix_second": mix_second}


def apply_sources(state, wet_col, wind_col, wind_rate, dissipation, mix_first, mix_second):
    low = state.astype(jnp.bfloat16)
    first = jnp.dot(mix_first, low, preferred_element_type=jnp.float32)
    second = jnp.dot(mix_second, low, preferred_element_type=jnp.float32)
    spread = jnp.sqrt(lax.optimization_barrier(jnp.mean(state * state, axis=0)) + 1e-06)
    growth = wind_rate[:, None] * wind_col * state + first * jax.nn.sigmoid(second) - dissipation[:, None] * spread * state
    return wet_col * (state + 0.5 * growth)

def reference(action, block_list, land_sea, ice, depth, current_x, current_y, wind, wind_rate, dissipation, mix_first, mix_second):
    wet = land_sea.astype(jnp.float32) * (1.0 - ice.astype(jnp.float32))
    bands = NY // RY
    table = block_list.reshape(bands, BAND_BLOCKS)
    band_rows = jnp.arange(bands, dtype=jnp.int32)[:, None] * RY + table // ROW_BLOCKS
    starts = band_rows * NX + table % ROW_BLOCKS * BLK
    cells = (starts[:, :, None] + jnp.arange(BLK, dtype=jnp.int32)[None, None, :]).reshape(-1).astype(jnp.int32)
    total = NY * NX
    place = jnp.zeros((total,), jnp.int32).at[cells].set(jnp.arange(total, dtype=jnp.int32))
    wet_col = jnp.take(wet.reshape(-1), cells)
    wind_col = jnp.take(wind.reshape(-1), cells)
    state = action * wet_col
    angle = 2.0 * math.pi * jnp.arange(ND, dtype=jnp.float32) / ND
    cosine = jnp.cos(angle)[:, None, None]
    sine = jnp.sin(angle)[:, None, None]

    def advect(operands):
        index, layer = operands
        frequency = index.astype(jnp.float32)
        speed = 0.4 * jnp.power(0.93, frequency) * jnp.tanh(depth * (1.0 + 0.25 * frequency))
        vel_x = wet * (speed * cosine + current_x)
        vel_y = wet * (speed * sine + current_y)
        field = layer.astype(jnp.float32)
        east = jnp.maximum(vel_x, 0.0) * field + jnp.minimum(jnp.roll(vel_x, -1, 2), 0.0) * jnp.roll(field, -1, 2)
        padded = jnp.pad(field, ((0, 0), (1, 1), (0, 0)))
        vel_pad = jnp.pad(vel_y, ((0, 0), (1, 1), (0, 0)))
        north = jnp.maximum(vel_pad[:, :-1], 0.0) * padded[:, :-1] + jnp.minimum(vel_pad[:, 1:], 0.0) * padded[:, 1:]
        moved = wet * (field - (east - jnp.roll(east, 1, 2)) - (north[:, 1:] - north[:, :-1]))
        return (moved - field).astype(jnp.bfloat16)
    count = BLK_DEV * BLK
    pieces = total // count

    def source_piece(index):
        start = index * count
        part_state = lax.dynamic_slice_in_dim(state_box[0], start, count, 1)
        part_wet = lax.dynamic_slice_in_dim(wet_col, start, count, 0)
        part_wind = lax.dynamic_slice_in_dim(wind_col, start, count, 0)
        return apply_sources(part_state, part_wet, part_wind, wind_rate, dissipation, mix_first, mix_second)
    for step in range(STEPS):
        low = state.astype(jnp.bfloat16)
        grid = jnp.take(low, place, axis=1).reshape(NF, ND, NY, NX)
        change = lax.map(advect, (jnp.arange(NF, dtype=jnp.int32), grid))
        state = state + jnp.take(change.reshape(K, total), cells, axis=1).astype(jnp.float32)
        state_box = [state]
        result = lax.map(source_piece, jnp.arange(pieces, dtype=jnp.int32))
        state = jnp.transpose(result, (1, 0, 2)).reshape(K, total)
    return state
```

```python
import functools
import math

import jax
import jax.numpy as jnp
import numpy as np
from jax import lax
from jax.experimental import pallas as pl
from jax.experimental.pallas import tpu as pltpu
from jax.sharding import PartitionSpec as P

ND = 36
K = 1296
TILE = 16
TILES = 81
BLK = 128
MEM = 16
BANDS = 8
SLOTS = 32
STEPS = 2
CHUNKS = 5
EXTRA = 5
HOT = 0
ZERO = 32
HALO = 33
FIELD = 49
MESH = pl.DeviceIdType.MESH
F32 = jnp.float32
BF16 = jnp.bfloat16


def component_table():
    index = np.arange(K)
    freq = (index // ND).astype(np.float64)
    angle = 2.0 * math.pi * (index % ND) / ND
    table = np.zeros((K, BLK), np.float32)
    table[:, 0] = 1.0 + 0.25 * freq
    table[:, 1] = 0.4 * 0.93**freq
    table[:, 2] = np.cos(angle)
    table[:, 3] = np.sin(angle)
    return table.reshape(TILES, TILE, BLK)


def kernel(
    bl, land, ice, depth, cur_x, cur_y, wind, wr, dis, cst, action, mix1, mix2,
    out,
    S, M1, M2, LOW, F1, F2, G, A, R, D, HO, HI, FE, FW, FN, FS, VX, VY, SM,
    MT, META, IDT, IDS, TBL, TBS, NB, C, WRB, DSB, OW, ACC,
    act_sem, mix_sem, cst_sem, tbl_sem, meta_send, meta_recv, id_send, id_recv,
    out_send, out_recv, halo_send, halo_recv, ret_send, ret_recv, fin_sem,
):
    band = lax.axis_index("band")
    me = lax.axis_index("grp")
    mx, my = me // 4, me % 4
    up, down = (band + 1) % BANDS, (band + BANDS - 1) % BANDS

    def peer(o):
        return ((mx + o // 4) % 4) * 4 + (my + o % 4) % 4

    def rows_of(t):
        return (1280, 16) if t == EXTRA else (256 * t, 256)

    order = [EXTRA] + list(range(CHUNKS))

    loads = {}
    for t in order:
        r0, n = rows_of(t)
        loads[t] = pltpu.make_async_copy(
            action.at[pl.ds(r0, n), pl.ds(0, 256)], S.at[pl.ds(r0, n)], act_sem.at[t]
        )
        loads[t].start()
    table_loads = []
    for t in range(CHUNKS + 1):
        tile = 80 if t == EXTRA else 16 * t + me
        table_loads.append(pltpu.make_async_copy(cst.at[tile], C.at[t], cst_sem.at[t]))
        table_loads[-1].start()
    mix_loads = [
        pltpu.make_async_copy(mix1, M1, mix_sem.at[0]),
        pltpu.make_async_copy(mix2, M2, mix_sem.at[1]),
    ]
    for one in mix_loads:
        one.start()

    barrier = pltpu.get_barrier_semaphore()

    def greet(o, carry):
        pl.semaphore_signal(barrier, inc=1, device_id=(band, peer(o)), device_id_type=MESH)
        return carry

    lax.fori_loop(1, MEM, greet, 0)
    pl.semaphore_signal(barrier, inc=1, device_id=(up, me), device_id_type=MESH)
    pl.semaphore_signal(barrier, inc=1, device_id=(down, me), device_id_type=MESH)

    wet = land[...].astype(F32) * (1.0 - ice[...].astype(F32))
    MT[0:4] = wet * depth[...]
    MT[4:8] = wet * cur_x[...]
    MT[8:12] = wet * cur_y[...]
    MT[12:16] = wind[...]
    IDT[...] = jnp.zeros_like(IDT)
    IDT[0:1] = jnp.full((1, BLK), bl[0], jnp.int32)
    IDT[1:2] = jnp.full((1, BLK), bl[1], jnp.int32)
    META[me] = MT[...]
    IDS[me] = IDT[...]
    for ref in (FE, FW, FN, FS):
        for par in range(2):
            ref[par, ZERO] = jnp.zeros((TILE, BLK), F32)

    pl.semaphore_wait(barrier, MEM + 1)

    def send_meta(o, carry):
        dst = peer(o)
        pltpu.make_async_remote_copy(
            src_ref=IDT, dst_ref=IDS.at[me], send_sem=id_send, recv_sem=id_recv,
            device_id=(band, dst), device_id_type=MESH,
        ).start()
        pltpu.make_async_remote_copy(
            src_ref=MT, dst_ref=META.at[me], send_sem=meta_send, recv_sem=meta_recv,
            device_id=(band, dst), device_id_type=MESH,
        ).start()
        return carry

    lax.fori_loop(1, MEM, send_meta, 0)

    def send_out(s, t):
        if t == EXTRA:
            @pl.when(me != HOT)
            def _():
                pltpu.make_async_remote_copy(
                    src_ref=G.at[s, 80], dst_ref=A.at[s, EXTRA, me],
                    send_sem=out_send.at[s, 1], recv_sem=out_recv.at[s, EXTRA],
                    device_id=(band, HOT), device_id_type=MESH,
                ).start()

            @pl.when(me == HOT)
            def _():
                A[s, EXTRA, HOT] = G[s, 80]
            return

        def one(o, carry):
            dst = peer(o)
            pltpu.make_async_remote_copy(
                src_ref=G.at[s, 16 * t + dst], dst_ref=A.at[s, t, me],
                send_sem=out_send.at[s, 0], recv_sem=out_recv.at[s, t],
                device_id=(band, dst), device_id_type=MESH,
            ).start()
            return carry

        lax.fori_loop(1, MEM, one, 0)
        A[s, t, me] = G[s, 16 * t + me]

    for t in order:
        r0, n = rows_of(t)
        loads[t].wait()

        def pack(i, carry, r0=r0):
            rows = pl.ds(pl.multiple_of(r0 + i * TILE, TILE), TILE)
            for sl in range(2):
                G[0, r0 // TILE + i, sl] = S[rows, sl * BLK:(sl + 1) * BLK].astype(BF16)
            return carry

        lax.fori_loop(0, n // TILE, pack, 0)
        send_out(0, t)

    def columns(i, carry):
        part = pl.ds(pl.multiple_of(i * BLK, BLK), BLK)
        diag = lax.broadcasted_iota(jnp.int32, (BLK, BLK), 0) == lax.broadcasted_iota(jnp.int32, (BLK, BLK), 1)
        for src, dst in ((wr, WRB), (dis, DSB)):
            col = jnp.sum(jnp.where(diag, src[0:1, part], 0.0), axis=1, keepdims=True)
            dst[part, :] = jnp.broadcast_to(col, (BLK, BLK))
        return carry

    lax.fori_loop(0, K // BLK, columns, 0)
    rest = K % BLK
    diag = lax.broadcasted_iota(jnp.int32, (rest, rest), 0) == lax.broadcasted_iota(jnp.int32, (rest, rest), 1)
    for src, dst in ((wr, WRB), (dis, DSB)):
        col = jnp.sum(jnp.where(diag, src[0:1, K - rest:K], 0.0), axis=1, keepdims=True)
        dst[K - rest:K, :] = jnp.broadcast_to(col, (rest, BLK))

    def wait_for(ref, sem):
        pltpu.make_async_copy(ref, ref, sem).wait()

    wait_for(IDS.at[pl.ds(0, MEM - 1)], id_recv)
    lane = lax.broadcasted_iota(jnp.int32, (1, BLK), 1)
    inverse = jnp.full((1, BLK), ZERO, jnp.int32)
    named = jnp.zeros((1, BLK), jnp.int32)
    for i in range(MEM):
        for sl in range(2):
            j = 2 * i + sl
            ident = IDS[i, sl:sl + 1, :]
            inverse = jnp.where(lane == ident + 16, j, inverse)
            named = jnp.where(lane == j, ident, named)
    inverse = jnp.where(lane < 16, HALO + lane, inverse)
    inverse = jnp.where(jnp.logical_and(lane >= 80, lane < 96), HALO + lane - 80, inverse)
    TBL[...] = jnp.zeros_like(TBL)
    TBL[0:1] = inverse
    TBL[1:2] = named
    to_smem = pltpu.make_async_copy(TBL, TBS, tbl_sem)
    to_smem.start()
    to_smem.wait()

    def neighbours(j, carry):
        q = TBS[1, j]
        line, place = (q // 16) * 16 + 16, q % 16
        NB[0, j] = TBS[0, line + (place + 15) % 16]
        NB[1, j] = TBS[0, line + (place + 1) % 16]
        NB[2, j] = TBS[0, q]
        NB[3, j] = TBS[0, q + 32]
        return carry

    lax.fori_loop(0, SLOTS, neighbours, 0)

    wait_for(META.at[pl.ds(0, MEM - 1)], meta_recv)

    def at_block(q):
        found = META[q % 16]
        r = q // 16
        pick = []
        for layer in range(4):
            got = found[4 * layer:4 * layer + 1]
            for k in range(1, 4):
                got = jnp.where(r == k, found[4 * layer + k:4 * layer + k + 1], got)
            pick.append(got)
        return pick

    def place_meta(j, carry):
        wd, wx, wy, _ = at_block(TBS[1, j])
        SM[j, 0:1] = wd
        SM[j, 1:2] = wx
        SM[j, 2:3] = wy
        SM[j, 3:4] = jnp.where(wd > 0.0, 1.0, 0.0)
        return carry

    lax.fori_loop(0, SLOTS, place_meta, 0)
    for sl in range(2):
        wd, _, _, wn = at_block(bl[sl])
        OW[0:1, sl * BLK:(sl + 1) * BLK] = jnp.where(wd > 0.0, 1.0, 0.0)
        OW[1:2, sl * BLK:(sl + 1) * BLK] = wn
    for one in table_loads:
        one.wait()

    lanes = lax.broadcasted_iota(jnp.int32, (TILE, BLK), 1)
    below = jnp.where(band > 0, 1.0, 0.0)
    above = jnp.where(band < BANDS - 1, 1.0, 0.0)

    def halo_copy(s, t, way):
        return pltpu.make_async_remote_copy(
            src_ref=HO.at[s, t, way], dst_ref=HI.at[s, t, way],
            send_sem=halo_send.at[s, t, way], recv_sem=halo_recv.at[s, t, way],
            device_id=(up if way == 0 else down, me), device_id_type=MESH,
        )

    def fluxes(s, t, par):
        count = MEM - 1
        wait_for(A.at[s, t, pl.ds(0, count)], out_recv.at[s, t])
        consts = C[t]
        aa, bb, cc, ss = (jnp.broadcast_to(consts[:, i:i + 1], (TILE, BLK)) for i in range(4))

        def one(i, carry):
            for sl in range(2):
                j = 2 * i + sl
                g = A[s, t, i, sl].astype(F32)
                if s == 0:
                    here = SM[j]
                    speed = bb * jnp.tanh(aa * here[0:1])
                    vx = speed * cc + here[1:2]
                    vy = speed * ss + here[2:3]
                    VX[t, j] = vx
                    VY[t, j] = vy
                else:
                    vx = VX[t, j]
                    vy = VY[t, j]
                px = vx * g
                east = jnp.where(vx > 0.0, px, 0.0)
                FE[par, j] = east
                FW[par, j] = east - px
                py = vy * g
                north = jnp.where(vy > 0.0, py, 0.0)
                FN[par, j] = north
                FS[par, j] = north - py
            return carry

        lax.fori_loop(0, MEM, one, 0, unroll=2)

        def edge(p, carry):
            HO[s, t, 0, p] = FN[par, TBS[0, 64 + p]].astype(BF16)
            HO[s, t, 1, p] = FS[par, TBS[0, 16 + p]].astype(BF16)
            return carry

        lax.fori_loop(0, MEM, edge, 0, unroll=2)
        halo_copy(s, t, 0).start()
        halo_copy(s, t, 1).start()

    def changes(s, t, par):
        halo_copy(s, t, 0).wait_recv()
        halo_copy(s, t, 1).wait_recv()

        def edge(p, carry):
            FN[par, HALO + p] = HI[s, t, 0, p].astype(F32) * below
            FS[par, HALO + p] = HI[s, t, 1, p].astype(F32) * above
            return carry

        lax.fori_loop(0, MEM, edge, 0, unroll=2)

        def one(i, carry):
            for sl in range(2):
                j = 2 * i + sl
                east, west = FE[par, j], FW[par, j]
                leaving = east + west + FN[par, j] + FS[par, j]
                come = FN[par, NB[2, j]] + FS[par, NB[3, j]]
                come += pltpu.roll(jnp.where(lanes == BLK - 1, FE[par, NB[0, j]], east), 1, 1)
                come += pltpu.roll(jnp.where(lanes == 0, FW[par, NB[1, j]], west), BLK - 1, 1)
                R[s, t, i, sl] = (SM[j, 3:4] * (come - leaving)).astype(BF16)
            return carry

        lax.fori_loop(0, MEM, one, 0, unroll=2)
        tile = 80 if t == EXTRA else 16 * t + me

        def send(o, carry):
            dst = peer(o)
            pltpu.make_async_remote_copy(
                src_ref=R.at[s, t, dst], dst_ref=D.at[s, tile],
                send_sem=ret_send.at[s, 1 if t == EXTRA else 0], recv_sem=ret_recv.at[s, t],
                device_id=(band, dst), device_id_type=MESH,
            ).start()
            return carry

        lax.fori_loop(1, MEM, send, 0)
        D[s, tile] = R[s, t, me]

    def combine(s, t):
        r0, n = rows_of(t)
        if t == EXTRA:
            @pl.when(me != HOT)
            def _():
                wait_for(D.at[s, 80], ret_recv.at[s, EXTRA])
        else:
            wait_for(D.at[s, pl.ds(16 * t, MEM - 1)], ret_recv.at[s, t])

        def one(i, carry):
            rows = pl.ds(pl.multiple_of(r0 + i * TILE, TILE), TILE)
            sums = []
            for sl in range(2):
                cols = slice(sl * BLK, (sl + 1) * BLK)
                x = S[rows, cols]
                if s == 0:
                    x = x * OW[0:1, cols]
                x = x + D[s, r0 // TILE + i, sl].astype(F32)
                S[rows, cols] = x
                LOW[rows, cols] = x.astype(BF16)
                sums.append(carry[sl] + x * x)
            return tuple(sums)

        got = lax.fori_loop(0, n // TILE, one, (ACC[0], ACC[1]), unroll=2 if n > TILE else 1)
        ACC[0], ACC[1] = got

    def source(s, t, spread):
        r0, n = rows_of(t)
        low = LOW[...]
        F1[0:n] = jnp.dot(M1[r0:r0 + n, :], low, preferred_element_type=F32)
        F2[0:n] = jnp.dot(M2[r0:r0 + n, :], low, preferred_element_type=F32)

        def one(i, carry):
            rows = pl.ds(pl.multiple_of(r0 + i * TILE, TILE), TILE)
            part = pl.ds(pl.multiple_of(i * TILE, TILE), TILE)
            for sl in range(2):
                cols = slice(sl * BLK, (sl + 1) * BLK)
                x = S[rows, cols]
                scale = 1.0 + 0.5 * (WRB[rows, :] * OW[1:2, cols] - DSB[rows, :] * spread[sl])
                x = OW[0:1, cols] * (x * scale + 0.25 * F1[part, cols] * (1.0 + jnp.tanh(0.5 * F2[part, cols])))
                S[rows, cols] = x
                if s == 0:
                    G[1, r0 // TILE + i, sl] = x.astype(BF16)
            return carry

        lax.fori_loop(0, n // TILE, one, 0, unroll=2 if n > TILE else 1)

    def result_copy(t):
        r0, n = rows_of(t)
        return pltpu.make_async_copy(S.at[pl.ds(r0, n)], out.at[pl.ds(r0, n)], fin_sem.at[t])

    for s in range(STEPS):
        @pl.when(me == HOT)
        def _():
            fluxes(s, EXTRA, 0)
        for t in range(CHUNKS):
            fluxes(s, t, (t + 1) % 2)
            if t == 0:
                @pl.when(me == HOT)
                def _():
                    changes(s, EXTRA, 0)
            else:
                changes(s, t - 1, t % 2)
        changes(s, CHUNKS - 1, CHUNKS % 2)

        ACC[...] = jnp.zeros_like(ACC)
        for t in order:
            combine(s, t)
        spread = [
            jnp.sqrt(jnp.sum(ACC[sl], axis=0, keepdims=True) * (1.0 / K) + 1e-06) for sl in range(2)
        ]
        if s == 0:
            for one in mix_loads:
                one.wait()
        for t in order:
            source(s, t, spread)
            if s == 0:
                send_out(1, t)
            else:
                result_copy(t).start()

    wait_for(IDS.at[pl.ds(0, MEM - 1)], id_send)
    wait_for(META.at[pl.ds(0, MEM - 1)], meta_send)
    for s in range(STEPS):
        wait_for(G.at[s, pl.ds(0, 75)], out_send.at[s, 0])
        wait_for(D.at[s, pl.ds(0, 75)], ret_send.at[s, 0])

        @pl.when(me != HOT)
        def _():
            wait_for(G.at[s, 80], out_send.at[s, 1])

        @pl.when(me == HOT)
        def _():
            wait_for(R.at[s, EXTRA, pl.ds(0, MEM - 1)], ret_send.at[s, 1])
            for way in range(2):
                halo_copy(s, EXTRA, way).wait_send()
        for t in range(CHUNKS):
            for way in range(2):
                halo_copy(s, t, way).wait_send()
    for t in order:
        result_copy(t).wait()


def on_device(action, block_list, land_sea, ice, depth, cur_x, cur_y, wind, wind_rate, dissipation, mix1, mix2):
    vmem = pl.BlockSpec(memory_space=pltpu.VMEM)
    hbm = pl.BlockSpec(memory_space=pl.ANY)
    smem = pl.BlockSpec(memory_space=pltpu.SMEM)
    dma = pltpu.SemaphoreType.DMA
    tile = (TILE, BLK)
    wet_part = pl.pallas_call(
        kernel,
        out_shape=jax.ShapeDtypeStruct((K, 256), F32),
        in_specs=[smem] + [vmem] * 8 + [hbm] * 4,
        out_specs=hbm,
        scratch_shapes=[
            pltpu.VMEM((K, 256), F32),
            pltpu.VMEM((K, K), BF16),
            pltpu.VMEM((K, K), BF16),
            pltpu.VMEM((K, 256), BF16),
            pltpu.VMEM((256, 256), F32),
            pltpu.VMEM((256, 256), F32),
            pltpu.VMEM((STEPS, TILES, 2) + tile, BF16),
            pltpu.VMEM((STEPS, 6, MEM, 2) + tile, BF16),
            pltpu.VMEM((STEPS, 6, MEM, 2) + tile, BF16),
            pltpu.VMEM((STEPS, TILES, 2) + tile, BF16),
            pltpu.VMEM((STEPS, 6, 2, MEM) + tile, BF16),
            pltpu.VMEM((STEPS, 6, 2, MEM) + tile, BF16),
            pltpu.VMEM((2, FIELD) + tile, F32),
            pltpu.VMEM((2, FIELD) + tile, F32),
            pltpu.VMEM((2, FIELD) + tile, F32),
            pltpu.VMEM((2, FIELD) + tile, F32),
            pltpu.VMEM((6, SLOTS) + tile, F32),
            pltpu.VMEM((6, SLOTS) + tile, F32),
            pltpu.VMEM((SLOTS, 8, BLK), F32),
            pltpu.VMEM((16, BLK), F32),
            pltpu.VMEM((MEM, 16, BLK), F32),
            pltpu.VMEM((8, BLK), jnp.int32),
            pltpu.VMEM((MEM, 8, BLK), jnp.int32),
            pltpu.VMEM((8, BLK), jnp.int32),
            pltpu.SMEM((8, BLK), jnp.int32),
            pltpu.SMEM((4, SLOTS), jnp.int32),
            pltpu.VMEM((6,) + tile, F32),
            pltpu.VMEM((K, BLK), F32),
            pltpu.VMEM((K, BLK), F32),
            pltpu.VMEM((8, 256), F32),
            pltpu.VMEM((2,) + tile, F32),
            dma((6,)), dma((2,)), dma((6,)), dma, dma, dma, dma, dma,
            dma((STEPS, 2)), dma((STEPS, 6)), dma((STEPS, 6, 2)), dma((STEPS, 6, 2)),
            dma((STEPS, 2)), dma((STEPS, 6)), dma((6,)),
        ],
        compiler_params=pltpu.CompilerParams(
            collective_id=0, has_side_effects=True, vmem_limit_bytes=48 * 1024 * 1024
        ),
        cost_estimate=pl.CostEstimate(flops=7 * 10**9, bytes_accessed=10**7, transcendentals=10**6),
    )(
        block_list, land_sea, ice, depth, cur_x, cur_y, wind,
        wind_rate.reshape(1, K), dissipation.reshape(1, K),
        jnp.asarray(component_table()), action, mix1, mix2,
    )
    return jnp.concatenate([wet_part, jnp.zeros((K, action.shape[1] - 256), F32)], axis=1)


def solution(mesh):
    col = P(None, ("band", "grp"))
    flat = P(("band", "grp"))
    grid = P("band", "grp")
    return jax.shard_map(
        on_device,
        mesh=mesh,
        in_specs=(col, flat, grid, grid, grid, grid, grid, grid, P(), P(), P(), P()),
        out_specs=col,
        check_vma=False,
    )
```

```python
import functools
import math

import jax
import jax.numpy as jnp
import numpy as np
from jax import lax
from jax.experimental import pallas as pl
from jax.experimental.pallas import tpu as pltpu
from jax.sharding import PartitionSpec as P

ND = 36
K = 1296
TILE = 16
TILES = 81
BLK = 128
MEM = 16
BANDS = 8
SLOTS = 32
STEPS = 2
CHUNKS = 5
EXTRA = 5
HOT = 0
ZERO = 32
HALO = 33
FIELD = 49
MESH = pl.DeviceIdType.MESH
F32 = jnp.float32
BF16 = jnp.bfloat16


def component_table():
    index = np.arange(K)
    freq = (index // ND).astype(np.float64)
    angle = 2.0 * math.pi * (index % ND) / ND
    table = np.zeros((K, BLK), np.float32)
    table[:, 0] = 1.0 + 0.25 * freq
    table[:, 1] = 0.4 * 0.93**freq
    table[:, 2] = np.cos(angle)
    table[:, 3] = np.sin(angle)
    return table.reshape(TILES, TILE, BLK)


def kernel(
    bl_in, land_in, ice_in, depth_in, cur_x_in, cur_y_in, wind_in, wr_in, dis_in, cst, action, mix1, mix2,
    out,
    bl, land, ice, depth, cur_x, cur_y, wind, wr, dis,
    S, M1, M2, LOW, F1, F2, G, A, R, D, HO, HI, NET, EDGE, FN, FS, VX, VY, SM,
    MT, META, IDT, IDS, TBL, TBS, NB, C, WRB, DSB, OW,
    small_sem, act_sem, mix_sem, cst_sem, tbl_sem, meta_send, meta_recv, id_send, id_recv,
    out_send, out_recv, halo_send, halo_recv, ret_send, ret_recv,
):
    band = lax.axis_index("band")
    me = lax.axis_index("grp")
    mx, my = me // 4, me % 4
    up, down = (band + 1) % BANDS, (band + BANDS - 1) % BANDS

    def peer(o):
        return ((mx + o // 4) % 4) * 4 + (my + o % 4) % 4

    def rows_of(t):
        return (1280, 16) if t == EXTRA else (256 * t, 256)

    order = [EXTRA] + list(range(CHUNKS))

    smalls = (
        (land_in, land), (ice_in, ice), (depth_in, depth), (cur_x_in, cur_x), (cur_y_in, cur_y),
        (wind_in, wind), (bl_in, bl), (wr_in, wr), (dis_in, dis),
    )
    small_loads = [pltpu.make_async_copy(a, c, small_sem.at[i]) for i, (a, c) in enumerate(smalls)]
    for one in small_loads:
        one.start()
    loads = {}
    for t in order:
        r0, n = rows_of(t)
        loads[t] = pltpu.make_async_copy(
            action.at[pl.ds(r0, n), pl.ds(0, 256)], S.at[pl.ds(r0, n)], act_sem.at[t]
        )
        loads[t].start()
    table_loads = []
    for t in range(CHUNKS + 1):
        tile = 80 if t == EXTRA else 16 * t + me
        table_loads.append(pltpu.make_async_copy(cst.at[tile], C.at[t], cst_sem.at[t]))
        table_loads[-1].start()
    mix_loads = [
        pltpu.make_async_copy(mix1, M1, mix_sem.at[0]),
        pltpu.make_async_copy(mix2, M2, mix_sem.at[1]),
    ]
    for one in mix_loads:
        one.start()

    barrier = pltpu.get_barrier_semaphore()

    def greet(o, carry):
        pl.semaphore_signal(barrier, inc=1, device_id=(band, peer(o)), device_id_type=MESH)
        return carry

    lax.fori_loop(1, MEM, greet, 0)
    pl.semaphore_signal(barrier, inc=1, device_id=(up, me), device_id_type=MESH)
    pl.semaphore_signal(barrier, inc=1, device_id=(down, me), device_id_type=MESH)

    for one in small_loads[:7]:
        one.wait()
    wet = land[...].astype(F32) * (1.0 - ice[...].astype(F32))
    MT[0:4] = wet * depth[...]
    MT[4:8] = wet * cur_x[...]
    MT[8:12] = wet * cur_y[...]
    MT[12:16] = wind[...]
    IDT[...] = jnp.zeros_like(IDT)
    IDT[0:1] = jnp.full((1, BLK), bl[0], jnp.int32)
    IDT[1:2] = jnp.full((1, BLK), bl[1], jnp.int32)
    META[me] = MT[...]
    IDS[me] = IDT[...]
    for ref in (EDGE, FN, FS):
        for par in range(2):
            ref[par, ZERO] = jnp.zeros((TILE, BLK), ref.dtype)

    pl.semaphore_wait(barrier, MEM + 1)

    def send_meta(o, carry):
        dst = peer(o)
        pltpu.make_async_remote_copy(
            src_ref=IDT, dst_ref=IDS.at[me], send_sem=id_send, recv_sem=id_recv,
            device_id=(band, dst), device_id_type=MESH,
        ).start()
        pltpu.make_async_remote_copy(
            src_ref=MT, dst_ref=META.at[me], send_sem=meta_send, recv_sem=meta_recv,
            device_id=(band, dst), device_id_type=MESH,
        ).start()
        return carry

    lax.fori_loop(1, MEM, send_meta, 0)

    def send_out(s, t):
        if t is EXTRA:
            @pl.when(me != HOT)
            def _():
                pltpu.make_async_remote_copy(
                    src_ref=G.at[s, 80], dst_ref=A.at[s, EXTRA, me],
                    send_sem=out_send.at[s, 1], recv_sem=out_recv.at[s, EXTRA],
                    device_id=(band, HOT), device_id_type=MESH,
                ).start()

            @pl.when(me == HOT)
            def _():
                A[s, EXTRA, HOT] = G[s, 80]
            return

        def one(o, carry):
            dst = peer(o)
            pltpu.make_async_remote_copy(
                src_ref=G.at[s, 16 * t + dst], dst_ref=A.at[s, t, me],
                send_sem=out_send.at[s, 0], recv_sem=out_recv.at[s, t],
                device_id=(band, dst), device_id_type=MESH,
            ).start()
            return carry

        lax.fori_loop(1, MEM, one, 0)
        A[s, t, me] = G[s, 16 * t + me]

    for t in order:
        r0, n = rows_of(t)
        loads[t].wait()

        def pack(i, carry, r0=r0):
            rows = pl.ds(pl.multiple_of(r0 + i * TILE, TILE), TILE)
            for sl in range(2):
                G[0, r0 // TILE + i, sl] = S[rows, sl * BLK:(sl + 1) * BLK].astype(BF16)
            return carry

        lax.fori_loop(0, n // TILE, pack, 0)
        send_out(0, t)

    for one in small_loads[7:]:
        one.wait()

    def columns(i, carry):
        part = pl.ds(pl.multiple_of(i * BLK, BLK), BLK)
        diag = lax.broadcasted_iota(jnp.int32, (BLK, BLK), 0) == lax.broadcasted_iota(jnp.int32, (BLK, BLK), 1)
        for src, dst in ((wr, WRB), (dis, DSB)):
            col = jnp.sum(jnp.where(diag, src[part].reshape(1, BLK), 0.0), axis=1, keepdims=True)
            dst[part, :] = jnp.broadcast_to(col, (BLK, BLK))
        return carry

    lax.fori_loop(0, K // BLK, columns, 0)
    rest = K % BLK
    diag = lax.broadcasted_iota(jnp.int32, (rest, rest), 0) == lax.broadcasted_iota(jnp.int32, (rest, rest), 1)
    for src, dst in ((wr, WRB), (dis, DSB)):
        col = jnp.sum(jnp.where(diag, src[K - rest:K].reshape(1, rest), 0.0), axis=1, keepdims=True)
        dst[K - rest:K, :] = jnp.broadcast_to(col, (rest, BLK))

    def wait_for(ref, sem):
        pltpu.make_async_copy(ref, ref, sem).wait()

    wait_for(IDS.at[pl.ds(0, MEM - 1)], id_recv)
    lane = lax.broadcasted_iota(jnp.int32, (1, BLK), 1)
    inverse = jnp.full((1, BLK), ZERO, jnp.int32)
    named = jnp.zeros((1, BLK), jnp.int32)
    for i in range(MEM):
        for sl in range(2):
            j = 2 * i + sl
            ident = IDS[i, sl:sl + 1, :]
            inverse = jnp.where(lane == ident + 16, j, inverse)
            named = jnp.where(lane == j, ident, named)
    inverse = jnp.where(lane < 16, jnp.where(band > 0, HALO + lane, ZERO), inverse)
    rim = jnp.where(band < BANDS - 1, HALO + lane - 80, ZERO)
    inverse = jnp.where(jnp.logical_and(lane >= 80, lane < 96), rim, inverse)
    TBL[...] = jnp.zeros_like(TBL)
    TBL[0:1] = inverse
    TBL[1:2] = named
    to_smem = pltpu.make_async_copy(TBL, TBS, tbl_sem)
    to_smem.start()
    to_smem.wait()

    def neighbours(j, carry):
        q = TBS[1, j]
        line, place = (q // 16) * 16 + 16, q % 16
        NB[0, j] = TBS[0, line + (place + 15) % 16]
        NB[1, j] = TBS[0, line + (place + 1) % 16]
        NB[2, j] = TBS[0, q]
        NB[3, j] = TBS[0, q + 32]
        return carry

    lax.fori_loop(0, SLOTS, neighbours, 0)

    wait_for(META.at[pl.ds(0, MEM - 1)], meta_recv)

    def at_block(q):
        found = META[q % 16]
        r = q // 16
        pick = []
        for layer in range(4):
            got = found[4 * layer:4 * layer + 1]
            for k in range(1, 4):
                got = jnp.where(r == k, found[4 * layer + k:4 * layer + k + 1], got)
            pick.append(got)
        return pick

    def place_meta(j, carry):
        wd, wx, wy, _ = at_block(TBS[1, j])
        SM[j, 0:1] = wd
        SM[j, 1:2] = wx
        SM[j, 2:3] = wy
        return carry

    lax.fori_loop(0, SLOTS, place_meta, 0)
    for sl in range(2):
        wd, _, _, wn = at_block(bl[sl])
        OW[0:1, sl * BLK:(sl + 1) * BLK] = jnp.where(wd > 0.0, 1.0, 0.0)
        OW[1:2, sl * BLK:(sl + 1) * BLK] = 0.5 * wn
    for one in table_loads:
        one.wait()

    lanes = lax.broadcasted_iota(jnp.int32, (TILE, BLK), 1)
    first_lane, last_lane = lanes == 0, lanes == BLK - 1

    def halo_copy(s, c, way):
        return pltpu.make_async_remote_copy(
            src_ref=HO.at[s, c, way], dst_ref=HI.at[s, c, way],
            send_sem=halo_send.at[s, c, way], recv_sem=halo_recv.at[s, c, way],
            device_id=(up if way == 0 else down, me), device_id_type=MESH,
        )

    def velocities(c):
        consts = C[c]
        aa, bb, cc, ss = (jnp.broadcast_to(consts[:, i:i + 1], (TILE, BLK)) for i in range(4))

        def one(j, carry):
            here = SM[j]
            speed = bb * jnp.tanh(aa * here[0:1])
            VX[c, j] = speed * cc + here[1:2]
            VY[c, j] = speed * ss + here[2:3]
            return carry

        lax.fori_loop(0, SLOTS, one, 0, unroll=8)

    def fluxes(s, c, par):
        if s == 0:
            velocities(c)
        wait_for(A.at[s, c, pl.ds(0, MEM - 1)], out_recv.at[s, c])

        def one(i, carry):
            for sl in range(2):
                j = 2 * i + sl
                g = A[s, c, i, sl].astype(F32)
                vx, vy = VX[c, j], VY[c, j]
                px, py = vx * g, vy * g
                east = jnp.where(vx > 0.0, px, 0.0)
                west = east - px
                north = jnp.where(vy > 0.0, py, 0.0)
                south = north - py
                from_west = pltpu.roll(east, 1, 1)
                from_east = pltpu.roll(west, BLK - 1, 1)
                inner = jnp.where(first_lane, 0.0, from_west) + jnp.where(last_lane, 0.0, from_east)
                NET[par, j] = inner - ((east + west) + (north + south))
                EDGE[par, j] = jnp.where(first_lane, from_west, from_east)
                FN[par, j] = north.astype(BF16)
                FS[par, j] = south.astype(BF16)
            return carry

        lax.fori_loop(0, MEM, one, 0, unroll=4)

        def edge(p, carry):
            HO[s, c, 0, p] = FN[par, TBS[0, 64 + p]]
            HO[s, c, 1, p] = FS[par, TBS[0, 16 + p]]
            return carry

        lax.fori_loop(0, MEM, edge, 0, unroll=4)
        halo_copy(s, c, 0).start()
        halo_copy(s, c, 1).start()

    def changes(s, c, par):
        halo_copy(s, c, 0).wait_recv()
        halo_copy(s, c, 1).wait_recv()
        FN[par, HALO:HALO + MEM] = HI[s, c, 0]
        FS[par, HALO:HALO + MEM] = HI[s, c, 1]

        def one(i, carry):
            for sl in range(2):
                j = 2 * i + sl
                sides = jnp.where(last_lane, EDGE[par, NB[1, j]], 0.0)
                sides = jnp.where(first_lane, EDGE[par, NB[0, j]], sides)
                lines = FN[par, NB[2, j]].astype(F32) + FS[par, NB[3, j]].astype(F32)
                R[s, c, i, sl] = (NET[par, j] + sides + lines).astype(BF16)
            return carry

        lax.fori_loop(0, MEM, one, 0, unroll=4)
        tile = 16 * c + me

        def send(o, carry):
            dst = peer(o)
            pltpu.make_async_remote_copy(
                src_ref=R.at[s, c, dst], dst_ref=D.at[s, tile],
                send_sem=ret_send.at[s, c], recv_sem=ret_recv.at[s, c],
                device_id=(band, dst), device_id_type=MESH,
            ).start()
            return carry

        lax.fori_loop(1, MEM, send, 0)
        D[s, tile] = R[s, c, me]

    def gather(s, r0, tiles, sums):
        def one(i, carry):
            rows = pl.ds(pl.multiple_of(r0 + i * TILE, TILE), TILE)
            new = []
            for sl in range(2):
                cols = slice(sl * BLK, (sl + 1) * BLK)
                x = S[rows, cols] + D[s, r0 // TILE + i, sl].astype(F32)
                S[rows, cols] = x
                LOW[rows, cols] = x.astype(BF16)
                new.append(carry[sl] + x * x)
            return tuple(new)

        return lax.fori_loop(0, tiles, one, sums, unroll=min(tiles, 4))

    def multiply(k0, depth, add):
        low = LOW[pl.ds(k0, depth), :]

        def one(i, carry):
            rows = pl.ds(pl.multiple_of(i * 432, 16), 432)
            for mix, total in ((M1, F1), (M2, F2)):
                got = jnp.dot(mix[rows, pl.ds(k0, depth)], low, preferred_element_type=F32)
                total[rows, :] = total[rows, :] + got if add else got
            return carry

        lax.fori_loop(0, 3, one, 0)

    def update(s, r0, tiles, spread):
        def one(i, carry):
            rows = pl.ds(pl.multiple_of(r0 + i * TILE, TILE), TILE)
            for sl in range(2):
                cols = slice(sl * BLK, (sl + 1) * BLK)
                scale = 1.0 + (WRB[rows, :] * OW[1:2, cols] - DSB[rows, :] * spread[sl])
                gated = 0.25 * F1[rows, cols] * (1.0 + jnp.tanh(0.5 * F2[rows, cols]))
                x = OW[0:1, cols] * (S[rows, cols] * scale + gated)
                if s == 0:
                    S[rows, cols] = x
                    G[1, r0 // TILE + i, sl] = x.astype(BF16)
                else:
                    out[rows, cols] = x
            return carry

        lax.fori_loop(0, tiles, one, 0, unroll=min(tiles, 4))

    start = jnp.where(me == HOT, -1, 0)
    for s in range(STEPS):
        def stage(i, carry, s=s):
            @pl.when(i < CHUNKS)
            def _():
                fluxes(s, jnp.where(i < 0, EXTRA, i), (i + 2) % 2)

            @pl.when(i > start)
            def _():
                changes(s, jnp.where(i < 1, EXTRA, i - 1), (i + 1) % 2)

            return carry

        lax.fori_loop(start, CHUNKS + 1, stage, 0)

        if s == 0:
            for one in mix_loads:
                one.wait()

        @pl.when(me != HOT)
        def _():
            wait_for(D.at[s, 80], ret_recv.at[s, EXTRA])

        zero = jnp.zeros((TILE, BLK), F32)
        sums = gather(s, 1280, 1, (zero, zero))
        multiply(1280, 16, False)

        def collect(t, sums, s=s):
            wait_for(D.at[s, pl.ds(16 * t, MEM - 1)], ret_recv.at[s, t])
            k0 = pl.multiple_of(t * 256, 256)
            sums = gather(s, k0, 16, sums)
            multiply(k0, 256, True)
            return sums

        sums = lax.fori_loop(0, CHUNKS, collect, sums)
        spread = [
            0.5 * jnp.sqrt(jnp.sum(one, axis=0, keepdims=True) * (1.0 / K) + 1e-06) for one in sums
        ]
        update(s, 1280, 1, spread)
        if s == 0:
            send_out(1, EXTRA)

        def finish(t, carry, s=s, spread=spread):
            update(s, pl.multiple_of(t * 256, 256), 16, spread)
            if s == 0:
                send_out(1, t)
            return carry

        lax.fori_loop(0, CHUNKS, finish, 0)

    wait_for(IDS.at[pl.ds(0, MEM - 1)], id_send)
    wait_for(META.at[pl.ds(0, MEM - 1)], meta_send)
    for s in range(STEPS):
        wait_for(G.at[s, pl.ds(0, 75)], out_send.at[s, 0])

        @pl.when(me != HOT)
        def _():
            wait_for(G.at[s, 80], out_send.at[s, 1])

        @pl.when(me == HOT)
        def _():
            wait_for(R.at[s, EXTRA, pl.ds(0, MEM - 1)], ret_send.at[s, EXTRA])
            for way in range(2):
                halo_copy(s, EXTRA, way).wait_send()
        for t in range(CHUNKS):
            wait_for(R.at[s, t, pl.ds(0, MEM - 1)], ret_send.at[s, t])
            for way in range(2):
                halo_copy(s, t, way).wait_send()


def on_device(action, block_list, land_sea, ice, depth, cur_x, cur_y, wind, wind_rate, dissipation, mix1, mix2):
    hbm = pl.BlockSpec(memory_space=pltpu.HBM)
    dma = pltpu.SemaphoreType.DMA
    tile = (TILE, BLK)

    def pinned(x):
        return pltpu.with_memory_space_constraint(x, pltpu.HBM)

    wet_part = pl.pallas_call(
        kernel,
        out_shape=pltpu.VMEM((K, 256), F32),
        in_specs=[hbm] * 13,
        out_specs=pl.BlockSpec(memory_space=pltpu.VMEM),
        scratch_shapes=[
            pltpu.SMEM((4,), jnp.int32),
            pltpu.VMEM((4, BLK), jnp.int32),
            pltpu.VMEM((4, BLK), jnp.int32),
            pltpu.VMEM((4, BLK), F32),
            pltpu.VMEM((4, BLK), F32),
            pltpu.VMEM((4, BLK), F32),
            pltpu.VMEM((4, BLK), F32),
            pltpu.VMEM((K,), F32),
            pltpu.VMEM((K,), F32),
            pltpu.VMEM((K, 256), F32),
            pltpu.VMEM((K, K), BF16),
            pltpu.VMEM((K, K), BF16),
            pltpu.VMEM((K, 256), BF16),
            pltpu.VMEM((K, 256), F32),
            pltpu.VMEM((K, 256), F32),
            pltpu.VMEM((STEPS, TILES, 2) + tile, BF16),
            pltpu.VMEM((STEPS, 6, MEM, 2) + tile, BF16),
            pltpu.VMEM((STEPS, 6, MEM, 2) + tile, BF16),
            pltpu.VMEM((STEPS, TILES, 2) + tile, BF16),
            pltpu.VMEM((STEPS, 6, 2, MEM) + tile, BF16),
            pltpu.VMEM((STEPS, 6, 2, MEM) + tile, BF16),
            pltpu.VMEM((2, SLOTS) + tile, F32),
            pltpu.VMEM((2, SLOTS + 1) + tile, F32),
            pltpu.VMEM((2, FIELD) + tile, BF16),
            pltpu.VMEM((2, FIELD) + tile, BF16),
            pltpu.VMEM((6, SLOTS) + tile, F32),
            pltpu.VMEM((6, SLOTS) + tile, F32),
            pltpu.VMEM((SLOTS, 8, BLK), F32),
            pltpu.VMEM((16, BLK), F32),
            pltpu.VMEM((MEM, 16, BLK), F32),
            pltpu.VMEM((8, BLK), jnp.int32),
            pltpu.VMEM((MEM, 8, BLK), jnp.int32),
            pltpu.VMEM((8, BLK), jnp.int32),
            pltpu.SMEM((8, BLK), jnp.int32),
            pltpu.SMEM((4, SLOTS), jnp.int32),
            pltpu.VMEM((6,) + tile, F32),
            pltpu.VMEM((K, BLK), F32),
            pltpu.VMEM((K, BLK), F32),
            pltpu.VMEM((8, 256), F32),
            dma((9,)), dma((6,)), dma((2,)), dma((6,)), dma, dma, dma, dma, dma,
            dma((STEPS, 2)), dma((STEPS, 6)), dma((STEPS, 6, 2)), dma((STEPS, 6, 2)),
            dma((STEPS, 6)), dma((STEPS, 6)),
        ],
        compiler_params=pltpu.CompilerParams(
            collective_id=0, has_side_effects=True, vmem_limit_bytes=48 * 1024 * 1024
        ),
        cost_estimate=pl.CostEstimate(flops=7 * 10**9, bytes_accessed=10**7, transcendentals=10**6),
    )(
        *(
            pinned(x)
            for x in (
                block_list, land_sea, ice, depth, cur_x, cur_y, wind, wind_rate, dissipation,
                jnp.asarray(component_table()), action, mix1, mix2,
            )
        ),
    )
    return jnp.concatenate([wet_part, jnp.zeros((K, action.shape[1] - 256), F32)], axis=1)


def solution(mesh):
    col = P(None, ("band", "grp"))
    flat = P(("band", "grp"))
    grid = P("band", "grp")
    return jax.shard_map(
        on_device,
        mesh=mesh,
        in_specs=(col, flat, grid, grid, grid, grid, grid, grid, P(), P(), P(), P()),
        out_specs=col,
        check_vma=False,
    )
```

```python
import functools
import math

import jax
import jax.numpy as jnp
import numpy as np
from jax import lax
from jax.experimental import pallas as pl
from jax.experimental.pallas import tpu as pltpu
from jax.sharding import PartitionSpec as P

ND = 36
K = 1296
TILE = 16
TILES = 81
BLK = 128
MEM = 16
BANDS = 8
SLOTS = 32
STEPS = 2
CHUNKS = 5
EXTRA = 5
HOT = 0
LAG = 3
BUFS = LAG + 1
ORDER = [(d // 4, d % 4) for d in range(1, 16)]
ZERO = 32
HALO = 33
FIELD = 49
MESH = pl.DeviceIdType.MESH
F32 = jnp.float32
BF16 = jnp.bfloat16


def component_table():
    index = np.arange(K)
    freq = (index // ND).astype(np.float64)
    angle = 2.0 * math.pi * (index % ND) / ND
    table = np.zeros((K, BLK), np.float32)
    table[:, 0] = 1.0 + 0.25 * freq
    table[:, 1] = 0.4 * 0.93**freq
    table[:, 2] = np.cos(angle)
    table[:, 3] = np.sin(angle)
    return table.reshape(TILES, TILE, BLK)


def kernel(
    bl_in, land_in, ice_in, depth_in, cur_x_in, cur_y_in, wind_in, wr_in, dis_in, cst, action, mix1, mix2,
    out,
    bl, land, ice, depth, cur_x, cur_y, wind, wr, dis,
    S, M1, M2, LOW, F1, F2, G, A, R, D, HO, HI, NET, EDGE, FN, FS, VX, VY, SM,
    MT, META, IDT, IDS, TBL, TBS, NB, C, WRB, DSB, OW,
    small_sem, act_sem, mix_sem, cst_sem, tbl_sem, meta_send, meta_recv, id_send, id_recv,
    out_send, out_recv, halo_send, halo_recv, ret_send, ret_recv,
):
    band = lax.axis_index("band")
    me = lax.axis_index("grp")
    up, down = lax.rem(band + 1, BANDS), lax.rem(band + BANDS - 1, BANDS)

    mx, my = lax.div(me, 4), lax.rem(me, 4)
    line_of = [4 * lax.rem(mx + d, 4) for d in range(4)]
    place_of = [lax.rem(my + d, 4) for d in range(4)]

    def each_peer(act):
        for dx, dy in ORDER:
            act(line_of[dx] + place_of[dy])

    def rows_of(t):
        return (1280, 16) if t == EXTRA else (256 * t, 256)

    order = [EXTRA] + list(range(CHUNKS))

    smalls = (
        (land_in, land), (ice_in, ice), (depth_in, depth), (cur_x_in, cur_x), (cur_y_in, cur_y),
        (wind_in, wind), (bl_in, bl), (wr_in, wr), (dis_in, dis),
    )
    small_loads = [pltpu.make_async_copy(a, c, small_sem.at[i]) for i, (a, c) in enumerate(smalls)]
    for one in small_loads:
        one.start()
    loads = {}
    for t in order:
        r0, n = rows_of(t)
        loads[t] = pltpu.make_async_copy(
            action.at[pl.ds(r0, n), pl.ds(0, 256)], S.at[pl.ds(r0, n)], act_sem.at[t]
        )
        loads[t].start()
    table_loads = []
    for t in range(CHUNKS + 1):
        tile = 80 if t == EXTRA else 16 * t + me
        table_loads.append(pltpu.make_async_copy(cst.at[tile], C.at[t], cst_sem.at[t]))
        table_loads[-1].start()
    mix_loads = [
        pltpu.make_async_copy(mix1, M1, mix_sem.at[0]),
        pltpu.make_async_copy(mix2, M2, mix_sem.at[1]),
    ]
    for one in mix_loads:
        one.start()

    barrier = pltpu.get_barrier_semaphore()

    def greet(dst):
        pl.semaphore_signal(barrier, inc=1, device_id=(band, dst), device_id_type=MESH)

    each_peer(greet)
    pl.semaphore_signal(barrier, inc=1, device_id=(up, me), device_id_type=MESH)
    pl.semaphore_signal(barrier, inc=1, device_id=(down, me), device_id_type=MESH)

    for one in small_loads[:7]:
        one.wait()
    wet = land[...].astype(F32) * (1.0 - ice[...].astype(F32))
    MT[0:4] = wet * depth[...]
    MT[4:8] = wet * cur_x[...]
    MT[8:12] = wet * cur_y[...]
    MT[12:16] = wind[...]
    IDT[...] = jnp.zeros_like(IDT)
    IDT[0:1] = jnp.full((1, BLK), bl[0], jnp.int32)
    IDT[1:2] = jnp.full((1, BLK), bl[1], jnp.int32)
    META[me] = MT[...]
    IDS[me] = IDT[...]
    for ref in (EDGE, FN, FS):
        for par in range(BUFS):
            ref[par, ZERO] = jnp.zeros((TILE, BLK), ref.dtype)

    pl.semaphore_wait(barrier, MEM + 1)

    def send_meta(dst):
        pltpu.make_async_remote_copy(
            src_ref=IDT, dst_ref=IDS.at[me], send_sem=id_send, recv_sem=id_recv,
            device_id=(band, dst), device_id_type=MESH,
        ).start()
        pltpu.make_async_remote_copy(
            src_ref=MT, dst_ref=META.at[me], send_sem=meta_send, recv_sem=meta_recv,
            device_id=(band, dst), device_id_type=MESH,
        ).start()

    each_peer(send_meta)

    def send_out(s, t):
        if t is EXTRA:
            @pl.when(me != HOT)
            def _():
                pltpu.make_async_remote_copy(
                    src_ref=G.at[s, 80], dst_ref=A.at[s, EXTRA, me],
                    send_sem=out_send.at[s, 1], recv_sem=out_recv.at[s, EXTRA],
                    device_id=(band, HOT), device_id_type=MESH,
                ).start()

            @pl.when(me == HOT)
            def _():
                A[s, EXTRA, HOT] = G[s, 80]
            return

        def one(dst):
            pltpu.make_async_remote_copy(
                src_ref=G.at[s, 16 * t + dst], dst_ref=A.at[s, t, me],
                send_sem=out_send.at[s, 0], recv_sem=out_recv.at[s, t],
                device_id=(band, dst), device_id_type=MESH,
            ).start()

        each_peer(one)
        A[s, t, me] = G[s, 16 * t + me]

    for t in order:
        r0, n = rows_of(t)
        loads[t].wait()

        def pack(i, carry, r0=r0):
            rows = pl.ds(pl.multiple_of(r0 + i * TILE, TILE), TILE)
            for sl in range(2):
                G[0, r0 // TILE + i, sl] = S[rows, sl * BLK:(sl + 1) * BLK].astype(BF16)
            return carry

        lax.fori_loop(0, n // TILE, pack, 0, unroll=min(n // TILE, 4))
        send_out(0, t)

    def rate_columns():
        for one in small_loads[7:]:
            one.wait()

        def columns(i, carry):
            part = pl.ds(pl.multiple_of(i * BLK, BLK), BLK)
            diag = lax.broadcasted_iota(jnp.int32, (BLK, BLK), 0) == lax.broadcasted_iota(jnp.int32, (BLK, BLK), 1)
            for src, dst in ((wr, WRB), (dis, DSB)):
                col = jnp.sum(jnp.where(diag, src[part].reshape(1, BLK), 0.0), axis=1, keepdims=True)
                dst[part, :] = jnp.broadcast_to(col, (BLK, BLK))
            return carry

        lax.fori_loop(0, K // BLK, columns, 0)
        rest = K % BLK
        diag = lax.broadcasted_iota(jnp.int32, (rest, rest), 0) == lax.broadcasted_iota(jnp.int32, (rest, rest), 1)
        for src, dst in ((wr, WRB), (dis, DSB)):
            col = jnp.sum(jnp.where(diag, src[K - rest:K].reshape(1, rest), 0.0), axis=1, keepdims=True)
            dst[K - rest:K, :] = jnp.broadcast_to(col, (rest, BLK))

    def wait_for(ref, sem):
        pltpu.make_async_copy(ref, ref, sem).wait()

    wait_for(IDS.at[pl.ds(0, MEM - 1)], id_recv)
    lane = lax.broadcasted_iota(jnp.int32, (1, BLK), 1)
    inverse = jnp.full((1, BLK), ZERO, jnp.int32)
    named = jnp.zeros((1, BLK), jnp.int32)
    for i in range(MEM):
        for sl in range(2):
            j = 2 * i + sl
            ident = IDS[i, sl:sl + 1, :]
            inverse = jnp.where(lane == ident + 16, j, inverse)
            named = jnp.where(lane == j, ident, named)
    inverse = jnp.where(lane < 16, jnp.where(band > 0, HALO + lane, ZERO), inverse)
    rim = jnp.where(band < BANDS - 1, HALO + lane - 80, ZERO)
    inverse = jnp.where(jnp.logical_and(lane >= 80, lane < 96), rim, inverse)
    TBL[...] = jnp.zeros_like(TBL)
    TBL[0:1] = inverse
    TBL[1:2] = named
    to_smem = pltpu.make_async_copy(TBL, TBS, tbl_sem)
    to_smem.start()
    to_smem.wait()

    def neighbours(j, carry):
        q = TBS[1, j]
        place = lax.rem(q, 16)
        line = q - place + 16
        NB[0, j] = TBS[0, line + lax.rem(place + 15, 16)]
        NB[1, j] = TBS[0, line + lax.rem(place + 1, 16)]
        NB[2, j] = TBS[0, q]
        NB[3, j] = TBS[0, q + 32]
        return carry

    lax.fori_loop(0, SLOTS, neighbours, 0, unroll=8)

    wait_for(META.at[pl.ds(0, MEM - 1)], meta_recv)

    def at_block(q):
        found = META[lax.rem(q, 16)]
        r = lax.div(q, 16)
        pick = []
        for layer in range(4):
            got = found[4 * layer:4 * layer + 1]
            for k in range(1, 4):
                got = jnp.where(r == k, found[4 * layer + k:4 * layer + k + 1], got)
            pick.append(got)
        return pick

    def place_meta(j, carry):
        wd, wx, wy, _ = at_block(TBS[1, j])
        SM[j, 0:1] = wd
        SM[j, 1:2] = wx
        SM[j, 2:3] = wy
        return carry

    lax.fori_loop(0, SLOTS, place_meta, 0, unroll=8)
    for sl in range(2):
        wd, _, _, wn = at_block(bl[sl])
        OW[0:1, sl * BLK:(sl + 1) * BLK] = jnp.where(wd > 0.0, 1.0, 0.0)
        OW[1:2, sl * BLK:(sl + 1) * BLK] = 0.5 * wn
    for one in table_loads:
        one.wait()

    lanes = lax.broadcasted_iota(jnp.int32, (TILE, BLK), 1)
    first_lane, last_lane = lanes == 0, lanes == BLK - 1

    def halo_copy(s, c, way):
        return pltpu.make_async_remote_copy(
            src_ref=HO.at[s, c, way], dst_ref=HI.at[s, c, way],
            send_sem=halo_send.at[s, c, way], recv_sem=halo_recv.at[s, c, way],
            device_id=(up if way == 0 else down, me), device_id_type=MESH,
        )

    def velocities(c):
        consts = C[c]
        aa, bb, cc, ss = (jnp.broadcast_to(consts[:, i:i + 1], (TILE, BLK)) for i in range(4))

        def one(j, carry):
            here = SM[j]
            speed = bb * jnp.tanh(aa * here[0:1])
            VX[c, j] = speed * cc + here[1:2]
            VY[c, j] = speed * ss + here[2:3]
            return carry

        lax.fori_loop(0, SLOTS, one, 0, unroll=8)

    def fluxes(s, c, par):
        if s == 0:
            velocities(c)
        wait_for(A.at[s, c, pl.ds(0, MEM - 1)], out_recv.at[s, c])

        def one(i, carry):
            for sl in range(2):
                j = 2 * i + sl
                g = A[s, c, i, sl].astype(F32)
                vx, vy = VX[c, j], VY[c, j]
                px, py = vx * g, vy * g
                east = jnp.where(vx > 0.0, px, 0.0)
                west = east - px
                north = jnp.where(vy > 0.0, py, 0.0)
                south = north - py
                from_west = pltpu.roll(east, 1, 1)
                from_east = pltpu.roll(west, BLK - 1, 1)
                inner = jnp.where(first_lane, 0.0, from_west) + jnp.where(last_lane, 0.0, from_east)
                NET[par, j] = inner - ((east + west) + (north + south))
                EDGE[par, j] = jnp.where(first_lane, from_west, from_east)
                FN[par, j] = north.astype(BF16)
                FS[par, j] = south.astype(BF16)
            return carry

        lax.fori_loop(0, MEM, one, 0, unroll=4)

        def edge(p, carry):
            HO[s, c, 0, p] = FN[par, TBS[0, 64 + p]]
            HO[s, c, 1, p] = FS[par, TBS[0, 16 + p]]
            return carry

        lax.fori_loop(0, MEM, edge, 0, unroll=4)
        halo_copy(s, c, 0).start()
        halo_copy(s, c, 1).start()

    def changes(s, c, par):
        halo_copy(s, c, 0).wait_recv()
        halo_copy(s, c, 1).wait_recv()
        FN[par, HALO:HALO + MEM] = HI[s, c, 0]
        FS[par, HALO:HALO + MEM] = HI[s, c, 1]

        def one(i, carry):
            for sl in range(2):
                j = 2 * i + sl
                sides = jnp.where(last_lane, EDGE[par, NB[1, j]], 0.0)
                sides = jnp.where(first_lane, EDGE[par, NB[0, j]], sides)
                lines = FN[par, NB[2, j]].astype(F32) + FS[par, NB[3, j]].astype(F32)
                R[s, c, i, sl] = (NET[par, j] + sides + lines).astype(BF16)
            return carry

        lax.fori_loop(0, MEM, one, 0, unroll=4)
        tile = 16 * c + me

        def send(dst):
            pltpu.make_async_remote_copy(
                src_ref=R.at[s, c, dst], dst_ref=D.at[s, tile],
                send_sem=ret_send.at[s, c], recv_sem=ret_recv.at[s, c],
                device_id=(band, dst), device_id_type=MESH,
            ).start()

        each_peer(send)
        D[s, tile] = R[s, c, me]

    def gather(s, r0, tiles, sums):
        def one(i, carry):
            rows = pl.ds(pl.multiple_of(r0 + i * TILE, TILE), TILE)
            new = []
            for sl in range(2):
                cols = slice(sl * BLK, (sl + 1) * BLK)
                x = S[rows, cols] + D[s, r0 // TILE + i, sl].astype(F32)
                S[rows, cols] = x
                LOW[rows, cols] = x.astype(BF16)
                new.append(carry[sl] + x * x)
            return tuple(new)

        return lax.fori_loop(0, tiles, one, sums, unroll=min(tiles, 4))

    def multiply(k0, depth, add):
        low = LOW[pl.ds(k0, depth), :]

        def one(i, carry):
            rows = pl.ds(pl.multiple_of(i * 432, 16), 432)
            for mix, total in ((M1, F1), (M2, F2)):
                got = jnp.dot(mix[rows, pl.ds(k0, depth)], low, preferred_element_type=F32)
                total[rows, :] = total[rows, :] + got if add else got
            return carry

        lax.fori_loop(0, 3, one, 0)

    def update(s, r0, tiles, spread):
        def one(i, carry):
            rows = pl.ds(pl.multiple_of(r0 + i * TILE, TILE), TILE)
            for sl in range(2):
                cols = slice(sl * BLK, (sl + 1) * BLK)
                scale = 1.0 + (WRB[rows, :] * OW[1:2, cols] - DSB[rows, :] * spread[sl])
                gated = 0.25 * F1[rows, cols] * (1.0 + jnp.tanh(0.5 * F2[rows, cols]))
                x = OW[0:1, cols] * (S[rows, cols] * scale + gated)
                if s == 0:
                    S[rows, cols] = x
                    G[1, r0 // TILE + i, sl] = x.astype(BF16)
                else:
                    out[rows, cols] = x
            return carry

        lax.fori_loop(0, tiles, one, 0, unroll=min(tiles, 4))

    start = jnp.where(me == HOT, -1, 0)
    for s in range(STEPS):
        def stage(i, carry, s=s):
            @pl.when(i < CHUNKS)
            def _():
                fluxes(s, jnp.where(i < 0, EXTRA, i), lax.rem(i + BUFS, BUFS))

            @pl.when(i > start + LAG - 1)
            def _():
                changes(s, jnp.where(i < LAG, EXTRA, i - LAG), lax.rem(i + BUFS - LAG, BUFS))

            return carry

        lax.fori_loop(start, CHUNKS + LAG, stage, 0)

        if s == 0:
            rate_columns()
            for one in mix_loads:
                one.wait()

        @pl.when(me != HOT)
        def _():
            wait_for(D.at[s, 80], ret_recv.at[s, EXTRA])

        zero = jnp.zeros((TILE, BLK), F32)
        sums = gather(s, 1280, 1, (zero, zero))
        multiply(1280, 16, False)

        def collect(t, sums, s=s):
            wait_for(D.at[s, pl.ds(16 * t, MEM - 1)], ret_recv.at[s, t])
            k0 = pl.multiple_of(t * 256, 256)
            sums = gather(s, k0, 16, sums)
            multiply(k0, 256, True)
            return sums

        sums = lax.fori_loop(0, CHUNKS, collect, sums)
        spread = [
            0.5 * jnp.sqrt(jnp.sum(one, axis=0, keepdims=True) * (1.0 / K) + 1e-06) for one in sums
        ]
        update(s, 1280, 1, spread)
        if s == 0:
            send_out(1, EXTRA)

        def finish(t, carry, s=s, spread=spread):
            update(s, pl.multiple_of(t * 256, 256), 16, spread)
            if s == 0:
                send_out(1, t)
            return carry

        lax.fori_loop(0, CHUNKS, finish, 0)

    wait_for(IDS.at[pl.ds(0, MEM - 1)], id_send)
    wait_for(META.at[pl.ds(0, MEM - 1)], meta_send)
    for s in range(STEPS):
        wait_for(G.at[s, pl.ds(0, 75)], out_send.at[s, 0])

        @pl.when(me != HOT)
        def _():
            wait_for(G.at[s, 80], out_send.at[s, 1])

        @pl.when(me == HOT)
        def _():
            wait_for(R.at[s, EXTRA, pl.ds(0, MEM - 1)], ret_send.at[s, EXTRA])
            for way in range(2):
                halo_copy(s, EXTRA, way).wait_send()
        for t in range(CHUNKS):
            wait_for(R.at[s, t, pl.ds(0, MEM - 1)], ret_send.at[s, t])
            for way in range(2):
                halo_copy(s, t, way).wait_send()


def on_device(action, block_list, land_sea, ice, depth, cur_x, cur_y, wind, wind_rate, dissipation, mix1, mix2):
    hbm = pl.BlockSpec(memory_space=pltpu.HBM)
    dma = pltpu.SemaphoreType.DMA
    tile = (TILE, BLK)

    def pinned(x):
        return pltpu.with_memory_space_constraint(x, pltpu.HBM)

    wet_part = pl.pallas_call(
        kernel,
        out_shape=pltpu.VMEM((K, 256), F32),
        in_specs=[hbm] * 13,
        out_specs=pl.BlockSpec(memory_space=pltpu.VMEM),
        scratch_shapes=[
            pltpu.SMEM((4,), jnp.int32),
            pltpu.VMEM((4, BLK), jnp.int32),
            pltpu.VMEM((4, BLK), jnp.int32),
            pltpu.VMEM((4, BLK), F32),
            pltpu.VMEM((4, BLK), F32),
            pltpu.VMEM((4, BLK), F32),
            pltpu.VMEM((4, BLK), F32),
            pltpu.VMEM((K,), F32),
            pltpu.VMEM((K,), F32),
            pltpu.VMEM((K, 256), F32),
            pltpu.VMEM((K, K), BF16),
            pltpu.VMEM((K, K), BF16),
            pltpu.VMEM((K, 256), BF16),
            pltpu.VMEM((K, 256), F32),
            pltpu.VMEM((K, 256), F32),
            pltpu.VMEM((STEPS, TILES, 2) + tile, BF16),
            pltpu.VMEM((STEPS, 6, MEM, 2) + tile, BF16),
            pltpu.VMEM((STEPS, 6, MEM, 2) + tile, BF16),
            pltpu.VMEM((STEPS, TILES, 2) + tile, BF16),
            pltpu.VMEM((STEPS, 6, 2, MEM) + tile, BF16),
            pltpu.VMEM((STEPS, 6, 2, MEM) + tile, BF16),
            pltpu.VMEM((BUFS, SLOTS) + tile, F32),
            pltpu.VMEM((BUFS, SLOTS + 1) + tile, F32),
            pltpu.VMEM((BUFS, FIELD) + tile, BF16),
            pltpu.VMEM((BUFS, FIELD) + tile, BF16),
            pltpu.VMEM((6, SLOTS) + tile, F32),
            pltpu.VMEM((6, SLOTS) + tile, F32),
            pltpu.VMEM((SLOTS, 8, BLK), F32),
            pltpu.VMEM((16, BLK), F32),
            pltpu.VMEM((MEM, 16, BLK), F32),
            pltpu.VMEM((8, BLK), jnp.int32),
            pltpu.VMEM((MEM, 8, BLK), jnp.int32),
            pltpu.VMEM((8, BLK), jnp.int32),
            pltpu.SMEM((8, BLK), jnp.int32),
            pltpu.SMEM((4, SLOTS), jnp.int32),
            pltpu.VMEM((6,) + tile, F32),
            pltpu.VMEM((K, BLK), F32),
            pltpu.VMEM((K, BLK), F32),
            pltpu.VMEM((8, 256), F32),
            dma((9,)), dma((6,)), dma((2,)), dma((6,)), dma, dma, dma, dma, dma,
            dma((STEPS, 2)), dma((STEPS, 6)), dma((STEPS, 6, 2)), dma((STEPS, 6, 2)),
            dma((STEPS, 6)), dma((STEPS, 6)),
        ],
        compiler_params=pltpu.CompilerParams(
            collective_id=0, has_side_effects=True, vmem_limit_bytes=48 * 1024 * 1024
        ),
        cost_estimate=pl.CostEstimate(flops=7 * 10**9, bytes_accessed=10**7, transcendentals=10**6),
    )(
        *(
            pinned(x)
            for x in (
                block_list, land_sea, ice, depth, cur_x, cur_y, wind, wind_rate, dissipation,
                jnp.asarray(component_table()), action, mix1, mix2,
            )
        ),
    )
    return jnp.concatenate([wet_part, jnp.zeros((K, action.shape[1] - 256), F32)], axis=1)


def solution(mesh):
    col = P(None, ("band", "grp"))
    flat = P(("band", "grp"))
    grid = P("band", "grp")
    return jax.shard_map(
        on_device,
        mesh=mesh,
        in_specs=(col, flat, grid, grid, grid, grid, grid, grid, P(), P(), P(), P()),
        out_specs=col,
        check_vma=False,
    )
```

```python
import functools
import math

import jax
import jax.numpy as jnp
import numpy as np
from jax import lax
from jax.experimental import pallas as pl
from jax.experimental.pallas import tpu as pltpu
from jax.sharding import PartitionSpec as P

ND = 36
K = 1296
TILE = 16
TILES = 81
BLK = 128
MEM = 16
BANDS = 8
SLOTS = 32
STEPS = 2
CHUNKS = 5
EXTRA = 5
HOT = 0
LAG = 3
BUFS = LAG + 1
ORDER = sorted([(d // 4, d % 4) for d in range(1, 16)], key=lambda d: -min(d[0], 4 - d[0]) - min(d[1], 4 - d[1]))
ZERO = 32
HALO = 33
FIELD = 49
MESH = pl.DeviceIdType.MESH
F32 = jnp.float32
BF16 = jnp.bfloat16


def component_table():
    index = np.arange(K)
    freq = (index // ND).astype(np.float64)
    angle = 2.0 * math.pi * (index % ND) / ND
    table = np.zeros((K, BLK), np.float32)
    table[:, 0] = 1.0 + 0.25 * freq
    table[:, 1] = 0.4 * 0.93**freq
    table[:, 2] = np.cos(angle)
    table[:, 3] = np.sin(angle)
    return table.reshape(TILES, TILE, BLK)


def sourced(S, F1, F2, WRB, DSB, OW, rows, sl):
    cols = slice(sl * BLK, (sl + 1) * BLK)
    scale = 1.0 + (WRB[rows, :] * OW[1:2, cols] - DSB[rows, :] * OW[2:3, cols])
    gated = F1[rows, cols] * (0.25 + 0.25 * jnp.tanh(0.5 * F2[rows, cols]))
    return OW[0:1, cols] * (S[rows, cols] * scale + gated)


def last_kernel(S, F1, F2, WRB, DSB, OW, out, made, zeros, made_sem, zero_sem):
    zeros[...] = jnp.zeros_like(zeros)
    part = K // 9
    for n in range(9):
        pltpu.make_async_copy(
            zeros, out.at[pl.ds(part * n, part), pl.ds(256, 256)], zero_sem.at[n]
        ).start()

    def copy_of(n):
        rows = pl.ds(part * n, part)
        return pltpu.make_async_copy(made.at[rows], out.at[rows, pl.ds(0, 256)], made_sem.at[n])

    for n in range(9):
        def one(i, carry, n=n):
            rows = pl.ds(pl.multiple_of(part * n + i * TILE, TILE), TILE)
            for sl in range(2):
                made[rows, sl * BLK:(sl + 1) * BLK] = sourced(S, F1, F2, WRB, DSB, OW, rows, sl)
            return carry

        lax.fori_loop(0, part // TILE, one, 0, unroll=3)
        copy_of(n).start()
    for n in range(9):
        pltpu.make_async_copy(
            zeros, out.at[pl.ds(part * n, part), pl.ds(256, 256)], zero_sem.at[n]
        ).wait()
        copy_of(n).wait()


def kernel(
    bl_in, land_in, ice_in, depth_in, cur_x_in, cur_y_in, wind_in, wr_in, dis_in, cst, action, mix1, mix2,
    S, F1, F2, WRB, DSB, OW,
    bl, land, ice, depth, cur_x, cur_y, wind, wr, dis,
    M1, M2, LOW, G, A, R, D, HO, HI, NET, EDGE, FN, FS, VX, VY, SM,
    MT, META, IDT, IDS, TBL, TBS, NB, C,
    small_sem, act_sem, mix_sem, cst_sem, tbl_sem, meta_send, meta_recv, id_send, id_recv,
    out_send, out_recv, halo_send, halo_recv, ret_send, ret_recv,
):
    band = lax.axis_index("band")
    me = lax.axis_index("grp")
    up, down = lax.rem(band + 1, BANDS), lax.rem(band + BANDS - 1, BANDS)

    mx, my = lax.div(me, 4), lax.rem(me, 4)
    line_of = [4 * lax.rem(mx + d, 4) for d in range(4)]
    place_of = [lax.rem(my + d, 4) for d in range(4)]

    def each_peer(act):
        for dx, dy in ORDER:
            act(line_of[dx] + place_of[dy])

    def rows_of(t):
        return (1280, 16) if t == EXTRA else (256 * t, 256)

    order = [EXTRA] + list(range(CHUNKS))

    smalls = (
        (land_in, land), (ice_in, ice), (depth_in, depth), (cur_x_in, cur_x), (cur_y_in, cur_y),
        (wind_in, wind), (bl_in, bl), (wr_in, wr), (dis_in, dis),
    )
    small_loads = [pltpu.make_async_copy(a, c, small_sem.at[i]) for i, (a, c) in enumerate(smalls)]
    for one in small_loads:
        one.start()
    loads = {}
    for t in order:
        r0, n = rows_of(t)
        loads[t] = pltpu.make_async_copy(
            action.at[pl.ds(r0, n), pl.ds(0, 256)], S.at[pl.ds(r0, n)], act_sem.at[t]
        )
        loads[t].start()
    table_loads = []
    for t in range(CHUNKS + 1):
        tile = 80 if t == EXTRA else 16 * t + me
        table_loads.append(pltpu.make_async_copy(cst.at[tile], C.at[t], cst_sem.at[t]))
        table_loads[-1].start()
    mix_loads = [
        pltpu.make_async_copy(mix1, M1, mix_sem.at[0]),
        pltpu.make_async_copy(mix2, M2, mix_sem.at[1]),
    ]
    for one in mix_loads:
        one.start()

    barrier = pltpu.get_barrier_semaphore()

    def greet(dst):
        pl.semaphore_signal(barrier, inc=1, device_id=(band, dst), device_id_type=MESH)

    each_peer(greet)
    pl.semaphore_signal(barrier, inc=1, device_id=(up, me), device_id_type=MESH)
    pl.semaphore_signal(barrier, inc=1, device_id=(down, me), device_id_type=MESH)

    for one in small_loads[:7]:
        one.wait()
    wet = land[...].astype(F32) * (1.0 - ice[...].astype(F32))
    MT[0:4] = wet * depth[...]
    MT[4:8] = wet * cur_x[...]
    MT[8:12] = wet * cur_y[...]
    MT[12:16] = wind[...]
    IDT[...] = jnp.zeros_like(IDT)
    IDT[0:1] = jnp.full((1, BLK), bl[0], jnp.int32)
    IDT[1:2] = jnp.full((1, BLK), bl[1], jnp.int32)
    META[me] = MT[...]
    IDS[me] = IDT[...]
    for ref in (EDGE, FN, FS):
        for par in range(BUFS):
            ref[par, ZERO] = jnp.zeros((TILE, BLK), ref.dtype)

    pl.semaphore_wait(barrier, MEM + 1)

    def send_meta(dst):
        pltpu.make_async_remote_copy(
            src_ref=IDT, dst_ref=IDS.at[me], send_sem=id_send, recv_sem=id_recv,
            device_id=(band, dst), device_id_type=MESH,
        ).start()
        pltpu.make_async_remote_copy(
            src_ref=MT, dst_ref=META.at[me], send_sem=meta_send, recv_sem=meta_recv,
            device_id=(band, dst), device_id_type=MESH,
        ).start()

    each_peer(send_meta)

    def send_out(s, t):
        if t is EXTRA:
            @pl.when(me != HOT)
            def _():
                pltpu.make_async_remote_copy(
                    src_ref=G.at[s, 80], dst_ref=A.at[s, EXTRA, me],
                    send_sem=out_send.at[s, 1], recv_sem=out_recv.at[s, EXTRA],
                    device_id=(band, HOT), device_id_type=MESH,
                ).start()

            @pl.when(me == HOT)
            def _():
                A[s, EXTRA, HOT] = G[s, 80]
            return

        def one(dst):
            pltpu.make_async_remote_copy(
                src_ref=G.at[s, 16 * t + dst], dst_ref=A.at[s, t, me],
                send_sem=out_send.at[s, 0], recv_sem=out_recv.at[s, t],
                device_id=(band, dst), device_id_type=MESH,
            ).start()

        each_peer(one)
        A[s, t, me] = G[s, 16 * t + me]

    for t in order:
        r0, n = rows_of(t)
        loads[t].wait()

        def pack(i, carry, r0=r0):
            rows = pl.ds(pl.multiple_of(r0 + i * TILE, TILE), TILE)
            for sl in range(2):
                G[0, r0 // TILE + i, sl] = S[rows, sl * BLK:(sl + 1) * BLK].astype(BF16)
            return carry

        lax.fori_loop(0, n // TILE, pack, 0, unroll=min(n // TILE, 4))
        send_out(0, t)

    def rate_columns():
        for one in small_loads[7:]:
            one.wait()

        def columns(i, carry):
            part = pl.ds(pl.multiple_of(i * BLK, BLK), BLK)
            diag = lax.broadcasted_iota(jnp.int32, (BLK, BLK), 0) == lax.broadcasted_iota(jnp.int32, (BLK, BLK), 1)
            for src, dst in ((wr, WRB), (dis, DSB)):
                col = jnp.sum(jnp.where(diag, src[part].reshape(1, BLK), 0.0), axis=1, keepdims=True)
                dst[part, :] = jnp.broadcast_to(col, (BLK, BLK))
            return carry

        lax.fori_loop(0, K // BLK, columns, 0)
        rest = K % BLK
        diag = lax.broadcasted_iota(jnp.int32, (rest, rest), 0) == lax.broadcasted_iota(jnp.int32, (rest, rest), 1)
        for src, dst in ((wr, WRB), (dis, DSB)):
            col = jnp.sum(jnp.where(diag, src[K - rest:K].reshape(1, rest), 0.0), axis=1, keepdims=True)
            dst[K - rest:K, :] = jnp.broadcast_to(col, (rest, BLK))

    def wait_for(ref, sem):
        pltpu.make_async_copy(ref, ref, sem).wait()

    wait_for(IDS.at[pl.ds(0, MEM - 1)], id_recv)
    lane = lax.broadcasted_iota(jnp.int32, (1, BLK), 1)
    inverse = jnp.full((1, BLK), ZERO, jnp.int32)
    named = jnp.zeros((1, BLK), jnp.int32)
    for i in range(MEM):
        for sl in range(2):
            j = 2 * i + sl
            ident = IDS[i, sl:sl + 1, :]
            inverse = jnp.where(lane == ident + 16, j, inverse)
            named = jnp.where(lane == j, ident, named)
    inverse = jnp.where(lane < 16, jnp.where(band > 0, HALO + lane, ZERO), inverse)
    rim = jnp.where(band < BANDS - 1, HALO + lane - 80, ZERO)
    inverse = jnp.where(jnp.logical_and(lane >= 80, lane < 96), rim, inverse)
    TBL[...] = jnp.zeros_like(TBL)
    TBL[0:1] = inverse
    TBL[1:2] = named
    to_smem = pltpu.make_async_copy(TBL, TBS, tbl_sem)
    to_smem.start()
    to_smem.wait()

    def neighbours(j, carry):
        q = TBS[1, j]
        place = lax.rem(q, 16)
        line = q - place + 16
        NB[0, j] = TBS[0, line + lax.rem(place + 15, 16)]
        NB[1, j] = TBS[0, line + lax.rem(place + 1, 16)]
        NB[2, j] = TBS[0, q]
        NB[3, j] = TBS[0, q + 32]
        return carry

    lax.fori_loop(0, SLOTS, neighbours, 0, unroll=8)

    wait_for(META.at[pl.ds(0, MEM - 1)], meta_recv)

    def at_block(q):
        found = META[lax.rem(q, 16)]
        r = lax.div(q, 16)
        pick = []
        for layer in range(4):
            got = found[4 * layer:4 * layer + 1]
            for k in range(1, 4):
                got = jnp.where(r == k, found[4 * layer + k:4 * layer + k + 1], got)
            pick.append(got)
        return pick

    def place_meta(j, carry):
        wd, wx, wy, _ = at_block(TBS[1, j])
        SM[j, 0:1] = wd
        SM[j, 1:2] = wx
        SM[j, 2:3] = wy
        return carry

    lax.fori_loop(0, SLOTS, place_meta, 0, unroll=8)
    for sl in range(2):
        wd, _, _, wn = at_block(bl[sl])
        OW[0:1, sl * BLK:(sl + 1) * BLK] = jnp.where(wd > 0.0, 1.0, 0.0)
        OW[1:2, sl * BLK:(sl + 1) * BLK] = 0.5 * wn
    for one in table_loads:
        one.wait()

    lanes = lax.broadcasted_iota(jnp.int32, (TILE, BLK), 1)
    first_lane, last_lane = lanes == 0, lanes == BLK - 1

    def halo_copy(s, c, way):
        return pltpu.make_async_remote_copy(
            src_ref=HO.at[s, c, way], dst_ref=HI.at[s, c, way],
            send_sem=halo_send.at[s, c, way], recv_sem=halo_recv.at[s, c, way],
            device_id=(up if way == 0 else down, me), device_id_type=MESH,
        )

    def velocities(c):
        consts = C[c]
        aa, bb, cc, ss = (jnp.broadcast_to(consts[:, i:i + 1], (TILE, BLK)) for i in range(4))

        def one(j, carry):
            here = SM[j]
            speed = bb * jnp.tanh(aa * here[0:1])
            VX[c, j] = speed * cc + here[1:2]
            VY[c, j] = speed * ss + here[2:3]
            return carry

        lax.fori_loop(0, SLOTS, one, 0, unroll=8)

    def fluxes(s, c, par):
        if s == 0:
            velocities(c)
        wait_for(A.at[s, c, pl.ds(0, MEM - 1)], out_recv.at[s, c])

        def one(i, carry):
            for sl in range(2):
                j = 2 * i + sl
                g = A[s, c, i, sl].astype(F32)
                vx, vy = VX[c, j], VY[c, j]
                px, py = vx * g, vy * g
                east = jnp.where(vx > 0.0, px, 0.0)
                west = east - px
                north = jnp.where(vy > 0.0, py, 0.0)
                south = north - py
                from_west = pltpu.roll(east, 1, 1)
                from_east = pltpu.roll(west, BLK - 1, 1)
                inner = jnp.where(first_lane, 0.0, from_west) + jnp.where(last_lane, 0.0, from_east)
                NET[par, j] = inner - ((east + west) + (north + south))
                EDGE[par, j] = jnp.where(first_lane, from_west, from_east)
                FN[par, j] = north.astype(BF16)
                FS[par, j] = south.astype(BF16)
            return carry

        lax.fori_loop(0, MEM, one, 0, unroll=8)

        def edge(p, carry):
            HO[s, c, 0, p] = FN[par, TBS[0, 64 + p]]
            HO[s, c, 1, p] = FS[par, TBS[0, 16 + p]]
            return carry

        lax.fori_loop(0, MEM, edge, 0, unroll=4)
        halo_copy(s, c, 0).start()
        halo_copy(s, c, 1).start()

    def changes(s, c, par):
        halo_copy(s, c, 0).wait_recv()
        halo_copy(s, c, 1).wait_recv()
        FN[par, HALO:HALO + MEM] = HI[s, c, 0]
        FS[par, HALO:HALO + MEM] = HI[s, c, 1]

        def one(i, carry):
            for sl in range(2):
                j = 2 * i + sl
                sides = jnp.where(last_lane, EDGE[par, NB[1, j]], 0.0)
                sides = jnp.where(first_lane, EDGE[par, NB[0, j]], sides)
                lines = FN[par, NB[2, j]].astype(F32) + FS[par, NB[3, j]].astype(F32)
                R[s, c, i, sl] = (NET[par, j] + sides + lines).astype(BF16)
            return carry

        lax.fori_loop(0, MEM, one, 0, unroll=8)
        tile = 16 * c + me

        def send(dst):
            pltpu.make_async_remote_copy(
                src_ref=R.at[s, c, dst], dst_ref=D.at[s, tile],
                send_sem=ret_send.at[s, c], recv_sem=ret_recv.at[s, c],
                device_id=(band, dst), device_id_type=MESH,
            ).start()

        each_peer(send)
        D[s, tile] = R[s, c, me]

    def gather(s, r0, tiles, sums):
        def one(i, carry):
            rows = pl.ds(pl.multiple_of(r0 + i * TILE, TILE), TILE)
            new = []
            for sl in range(2):
                cols = slice(sl * BLK, (sl + 1) * BLK)
                x = S[rows, cols] + D[s, r0 // TILE + i, sl].astype(F32)
                S[rows, cols] = x
                LOW[rows, cols] = x.astype(BF16)
                new.append(carry[sl] + x * x)
            return tuple(new)

        return lax.fori_loop(0, tiles, one, sums, unroll=min(tiles, 4))

    def multiply(k0, depth, add):
        low = LOW[pl.ds(k0, depth), :]

        def one(i, carry):
            rows = pl.ds(pl.multiple_of(i * 432, 16), 432)
            for mix, total in ((M1, F1), (M2, F2)):
                got = jnp.dot(mix[rows, pl.ds(k0, depth)], low, preferred_element_type=F32)
                total[rows, :] = total[rows, :] + got if add else got
            return carry

        lax.fori_loop(0, 3, one, 0)

    def update(r0, tiles):
        def one(i, carry):
            rows = pl.ds(pl.multiple_of(r0 + i * TILE, TILE), TILE)
            for sl in range(2):
                x = sourced(S, F1, F2, WRB, DSB, OW, rows, sl)
                S[rows, sl * BLK:(sl + 1) * BLK] = x
                G[1, r0 // TILE + i, sl] = x.astype(BF16)
            return carry

        lax.fori_loop(0, tiles, one, 0, unroll=min(tiles, 4))

    start = jnp.where(me == HOT, -1, 0)
    for s in range(STEPS):
        def stage(i, carry, s=s):
            @pl.when(i < CHUNKS)
            def _():
                fluxes(s, jnp.where(i < 0, EXTRA, i), lax.rem(i + BUFS, BUFS))

            @pl.when(i > start + LAG - 1)
            def _():
                changes(s, jnp.where(i < LAG, EXTRA, i - LAG), lax.rem(i + BUFS - LAG, BUFS))

            return carry

        lax.fori_loop(start, CHUNKS + LAG, stage, 0)

        if s == 0:
            rate_columns()
            for one in mix_loads:
                one.wait()

        @pl.when(me != HOT)
        def _():
            wait_for(D.at[s, 80], ret_recv.at[s, EXTRA])

        zero = jnp.zeros((TILE, BLK), F32)
        sums = gather(s, 1280, 1, (zero, zero))
        multiply(1280, 16, False)

        def collect(t, sums, s=s):
            wait_for(D.at[s, pl.ds(16 * t, MEM - 1)], ret_recv.at[s, t])
            k0 = pl.multiple_of(t * 256, 256)
            sums = gather(s, k0, 16, sums)
            multiply(k0, 256, True)
            return sums

        sums = lax.fori_loop(0, CHUNKS, collect, sums)
        for sl in range(2):
            mean = jnp.sum(sums[sl], axis=0, keepdims=True) * (1.0 / K)
            OW[2:3, sl * BLK:(sl + 1) * BLK] = 0.5 * jnp.sqrt(mean + 1e-06)

        if s == 0:
            update(1280, 1)
            send_out(1, EXTRA)

            def finish(t, carry):
                update(pl.multiple_of(t * 256, 256), 16)
                send_out(1, t)
                return carry

            lax.fori_loop(0, CHUNKS, finish, 0)

    wait_for(IDS.at[pl.ds(0, MEM - 1)], id_send)
    wait_for(META.at[pl.ds(0, MEM - 1)], meta_send)
    for s in range(STEPS):
        wait_for(G.at[s, pl.ds(0, 75)], out_send.at[s, 0])

        @pl.when(me != HOT)
        def _():
            wait_for(G.at[s, 80], out_send.at[s, 1])

        @pl.when(me == HOT)
        def _():
            wait_for(R.at[s, EXTRA, pl.ds(0, MEM - 1)], ret_send.at[s, EXTRA])
            for way in range(2):
                halo_copy(s, EXTRA, way).wait_send()
        for t in range(CHUNKS):
            wait_for(R.at[s, t, pl.ds(0, MEM - 1)], ret_send.at[s, t])
            for way in range(2):
                halo_copy(s, t, way).wait_send()


def on_device(action, block_list, land_sea, ice, depth, cur_x, cur_y, wind, wind_rate, dissipation, mix1, mix2):
    hbm = pl.BlockSpec(memory_space=pltpu.HBM)
    dma = pltpu.SemaphoreType.DMA
    tile = (TILE, BLK)

    def pinned(x):
        return pltpu.with_memory_space_constraint(x, pltpu.HBM)

    state = pl.pallas_call(
        kernel,
        out_shape=[
            pltpu.VMEM((K, 256), F32),
            pltpu.VMEM((K, 256), F32),
            pltpu.VMEM((K, 256), F32),
            pltpu.VMEM((K, BLK), F32),
            pltpu.VMEM((K, BLK), F32),
            pltpu.VMEM((8, 256), F32),
        ],
        in_specs=[hbm] * 13,
        out_specs=[pl.BlockSpec(memory_space=pltpu.VMEM)] * 6,
        scratch_shapes=[
            pltpu.SMEM((4,), jnp.int32),
            pltpu.VMEM((4, BLK), jnp.int32),
            pltpu.VMEM((4, BLK), jnp.int32),
            pltpu.VMEM((4, BLK), F32),
            pltpu.VMEM((4, BLK), F32),
            pltpu.VMEM((4, BLK), F32),
            pltpu.VMEM((4, BLK), F32),
            pltpu.VMEM((K,), F32),
            pltpu.VMEM((K,), F32),
            pltpu.VMEM((K, K), BF16),
            pltpu.VMEM((K, K), BF16),
            pltpu.VMEM((K, 256), BF16),
            pltpu.VMEM((STEPS, TILES, 2) + tile, BF16),
            pltpu.VMEM((STEPS, 6, MEM, 2) + tile, BF16),
            pltpu.VMEM((STEPS, 6, MEM, 2) + tile, BF16),
            pltpu.VMEM((STEPS, TILES, 2) + tile, BF16),
            pltpu.VMEM((STEPS, 6, 2, MEM) + tile, BF16),
            pltpu.VMEM((STEPS, 6, 2, MEM) + tile, BF16),
            pltpu.VMEM((BUFS, SLOTS) + tile, F32),
            pltpu.VMEM((BUFS, SLOTS + 1) + tile, F32),
            pltpu.VMEM((BUFS, FIELD) + tile, BF16),
            pltpu.VMEM((BUFS, FIELD) + tile, BF16),
            pltpu.VMEM((6, SLOTS) + tile, F32),
            pltpu.VMEM((6, SLOTS) + tile, F32),
            pltpu.VMEM((SLOTS, 8, BLK), F32),
            pltpu.VMEM((16, BLK), F32),
            pltpu.VMEM((MEM, 16, BLK), F32),
            pltpu.VMEM((8, BLK), jnp.int32),
            pltpu.VMEM((MEM, 8, BLK), jnp.int32),
            pltpu.VMEM((8, BLK), jnp.int32),
            pltpu.SMEM((8, BLK), jnp.int32),
            pltpu.SMEM((4, SLOTS), jnp.int32),
            pltpu.VMEM((6,) + tile, F32),
            dma((9,)), dma((6,)), dma((2,)), dma((6,)), dma, dma, dma, dma, dma,
            dma((STEPS, 2)), dma((STEPS, 6)), dma((STEPS, 6, 2)), dma((STEPS, 6, 2)),
            dma((STEPS, 6)), dma((STEPS, 6)),
        ],
        compiler_params=pltpu.CompilerParams(
            collective_id=0, has_side_effects=True, vmem_limit_bytes=48 * 1024 * 1024
        ),
        cost_estimate=pl.CostEstimate(flops=7 * 10**9, bytes_accessed=10**7, transcendentals=10**6),
    )(
        *(
            pinned(x)
            for x in (
                block_list, land_sea, ice, depth, cur_x, cur_y, wind, wind_rate, dissipation,
                jnp.asarray(component_table()), action, mix1, mix2,
            )
        ),
    )
    return pl.pallas_call(
        last_kernel,
        out_shape=jax.ShapeDtypeStruct(action.shape, F32),
        in_specs=[pl.BlockSpec(memory_space=pltpu.VMEM)] * 6,
        out_specs=hbm,
        scratch_shapes=[
            pltpu.VMEM((K, 256), F32),
            pltpu.VMEM((K // 9, 256), F32),
            dma((9,)), dma((9,)),
        ],
        compiler_params=pltpu.CompilerParams(vmem_limit_bytes=8 * 1024 * 1024),
    )(*state)


def solution(mesh):
    col = P(None, ("band", "grp"))
    flat = P(("band", "grp"))
    grid = P("band", "grp")
    return jax.shard_map(
        on_device,
        mesh=mesh,
        in_specs=(col, flat, grid, grid, grid, grid, grid, grid, P(), P(), P(), P()),
        out_specs=col,
        check_vma=False,
    )
```

```python
import functools
import math

import jax
import jax.numpy as jnp
import numpy as np
from jax import lax
from jax.experimental import pallas as pl
from jax.experimental.pallas import tpu as pltpu
from jax.sharding import PartitionSpec as P

ND = 36
K = 1296
TILE = 16
TILES = 81
BLK = 128
MEM = 16
BANDS = 8
SLOTS = 32
STEPS = 2
CHUNKS = 5
EXTRA = 5
HOT = 0
LAG = 3
BUFS = LAG + 1
ORDER = sorted([(d // 4, d % 4) for d in range(1, 16)], key=lambda d: -min(d[0], 4 - d[0]) - min(d[1], 4 - d[1]))
ZERO = 32
HALO = 33
FIELD = 49
MESH = pl.DeviceIdType.MESH
F32 = jnp.float32
BF16 = jnp.bfloat16


def component_table():
    index = np.arange(K)
    freq = (index // ND).astype(np.float64)
    angle = 2.0 * math.pi * (index % ND) / ND
    table = np.zeros((K, BLK), np.float32)
    table[:, 0] = 1.0 + 0.25 * freq
    table[:, 1] = 0.4 * 0.93**freq
    table[:, 2] = np.cos(angle)
    table[:, 3] = np.sin(angle)
    return table.reshape(TILES, TILE, BLK)


def sourced(S, F1, F2, WRB, DSB, OW, rows, sl):
    cols = slice(sl * BLK, (sl + 1) * BLK)
    scale = 1.0 + (WRB[rows, :] * OW[1:2, cols] - DSB[rows, :] * OW[2:3, cols])
    gated = F1[rows, cols] * (0.25 + 0.25 * jnp.tanh(0.5 * F2[rows, cols]))
    return OW[0:1, cols] * (S[rows, cols] * scale + gated)


def last_kernel(S, F1, F2, WRB, DSB, OW, out, made, zeros, made_sem, zero_sem):
    zeros[...] = jnp.zeros_like(zeros)
    part = K // 9
    for n in range(9):
        pltpu.make_async_copy(
            zeros, out.at[pl.ds(part * n, part), pl.ds(256, 256)], zero_sem.at[n]
        ).start()

    def copy_of(n):
        rows = pl.ds(part * n, part)
        return pltpu.make_async_copy(made.at[rows], out.at[rows, pl.ds(0, 256)], made_sem.at[n])

    for n in range(9):
        def one(i, carry, n=n):
            rows = pl.ds(pl.multiple_of(part * n + i * TILE, TILE), TILE)
            for sl in range(2):
                made[rows, sl * BLK:(sl + 1) * BLK] = sourced(S, F1, F2, WRB, DSB, OW, rows, sl)
            return carry

        lax.fori_loop(0, part // TILE, one, 0, unroll=3)
        copy_of(n).start()
    for n in range(9):
        pltpu.make_async_copy(
            zeros, out.at[pl.ds(part * n, part), pl.ds(256, 256)], zero_sem.at[n]
        ).wait()
        copy_of(n).wait()


def kernel(
    bl_in, land_in, ice_in, depth_in, cur_x_in, cur_y_in, wind_in, wr_in, dis_in, cst, action, mix1, mix2,
    S, F1, F2, WRB, DSB, OW,
    bl, land, ice, depth, cur_x, cur_y, wind, wr, dis,
    M1, M2, LOW, G, A, R, D, HO, HI, NET, EDGE, FN, FS, VX, VY, SM,
    MT, META, WND, IDT, IDS, TBL, TBS, NB, C,
    small_sem, act_sem, mix_sem, cst_sem, tbl_sem, meta_send, meta_recv, id_send, id_recv, wind_send, wind_recv,
    out_send, out_recv, halo_send, halo_recv, ret_send, ret_recv,
):
    band = lax.axis_index("band")
    me = lax.axis_index("grp")
    up, down = lax.rem(band + 1, BANDS), lax.rem(band + BANDS - 1, BANDS)

    mx, my = lax.div(me, 4), lax.rem(me, 4)
    line_of = [4 * lax.rem(mx + d, 4) for d in range(4)]
    place_of = [lax.rem(my + d, 4) for d in range(4)]

    def each_peer(act):
        for dx, dy in ORDER:
            act(line_of[dx] + place_of[dy])

    def rows_of(t):
        return (1280, 16) if t == EXTRA else (256 * t, 256)

    order = [EXTRA] + list(range(CHUNKS))

    smalls = (
        (land_in, land), (ice_in, ice), (depth_in, depth), (cur_x_in, cur_x), (cur_y_in, cur_y),
        (wind_in, wind), (bl_in, bl), (wr_in, wr), (dis_in, dis),
    )
    small_loads = [pltpu.make_async_copy(a, c, small_sem.at[i]) for i, (a, c) in enumerate(smalls)]
    for one in small_loads:
        one.start()
    loads = {}
    for t in order:
        r0, n = rows_of(t)
        loads[t] = pltpu.make_async_copy(
            action.at[pl.ds(r0, n), pl.ds(0, 256)], S.at[pl.ds(r0, n)], act_sem.at[t]
        )
        loads[t].start()
    table_loads = []
    for t in range(CHUNKS + 1):
        tile = 80 if t == EXTRA else 16 * t + me
        table_loads.append(pltpu.make_async_copy(cst.at[tile], C.at[t], cst_sem.at[t]))
        table_loads[-1].start()
    mix_loads = [
        pltpu.make_async_copy(mix1, M1, mix_sem.at[0]),
        pltpu.make_async_copy(mix2, M2, mix_sem.at[1]),
    ]
    for one in mix_loads:
        one.start()

    barrier = pltpu.get_barrier_semaphore()

    def greet(dst):
        pl.semaphore_signal(barrier, inc=1, device_id=(band, dst), device_id_type=MESH)

    each_peer(greet)
    pl.semaphore_signal(barrier, inc=1, device_id=(up, me), device_id_type=MESH)
    pl.semaphore_signal(barrier, inc=1, device_id=(down, me), device_id_type=MESH)

    for one in small_loads[:7]:
        one.wait()
    wet = land[...].astype(F32) * (1.0 - ice[...].astype(F32))
    MT[0] = wet * depth[...]
    MT[1] = wet * cur_x[...]
    MT[2] = wet * cur_y[...]
    IDT[0:1] = jnp.full((1, BLK), bl[0], jnp.int32)
    IDT[1:2] = jnp.full((1, BLK), bl[1], jnp.int32)
    META[me] = MT[...]
    IDS[me] = IDT[...]
    WND[me] = wind[...]
    for ref in (EDGE, FN, FS):
        for par in range(BUFS):
            ref[par, ZERO] = jnp.zeros((TILE, BLK), ref.dtype)

    pl.semaphore_wait(barrier, MEM + 1)

    def send_meta(dst):
        pltpu.make_async_remote_copy(
            src_ref=IDT, dst_ref=IDS.at[me], send_sem=id_send, recv_sem=id_recv,
            device_id=(band, dst), device_id_type=MESH,
        ).start()
        pltpu.make_async_remote_copy(
            src_ref=MT, dst_ref=META.at[me], send_sem=meta_send, recv_sem=meta_recv,
            device_id=(band, dst), device_id_type=MESH,
        ).start()

    each_peer(send_meta)

    def send_out(s, t):
        if t is EXTRA:
            @pl.when(me != HOT)
            def _():
                pltpu.make_async_remote_copy(
                    src_ref=G.at[s, 80], dst_ref=A.at[s, EXTRA, me],
                    send_sem=out_send.at[s, 1], recv_sem=out_recv.at[s, EXTRA],
                    device_id=(band, HOT), device_id_type=MESH,
                ).start()

            @pl.when(me == HOT)
            def _():
                A[s, EXTRA, HOT] = G[s, 80]
            return

        def one(dst):
            pltpu.make_async_remote_copy(
                src_ref=G.at[s, 16 * t + dst], dst_ref=A.at[s, t, me],
                send_sem=out_send.at[s, 0], recv_sem=out_recv.at[s, t],
                device_id=(band, dst), device_id_type=MESH,
            ).start()

        each_peer(one)
        A[s, t, me] = G[s, 16 * t + me]

    def wait_for(ref, sem):
        pltpu.make_async_copy(ref, ref, sem).wait()

    def first_out(t):
        r0, n = rows_of(t)
        loads[t].wait()

        def pack(i, carry):
            rows = pl.ds(pl.multiple_of(r0 + i * TILE, TILE), TILE)
            for sl in range(2):
                G[0, r0 // TILE + i, sl] = S[rows, sl * BLK:(sl + 1) * BLK].astype(BF16)
            return carry

        lax.fori_loop(0, n // TILE, pack, 0, unroll=min(n // TILE, 4))
        send_out(0, t)

    for t in order[:3]:
        first_out(t)

    wait_for(IDS.at[pl.ds(0, MEM - 1)], id_recv)
    lane = lax.broadcasted_iota(jnp.int32, (1, BLK), 1)
    inverse = jnp.full((1, BLK), ZERO, jnp.int32)
    named = jnp.zeros((1, BLK), jnp.int32)
    for i in range(MEM):
        for sl in range(2):
            j = 2 * i + sl
            ident = IDS[i, sl:sl + 1, :]
            inverse = jnp.where(lane == ident + 16, j, inverse)
            named = jnp.where(lane == j, ident, named)
    inverse = jnp.where(lane < 16, jnp.where(band > 0, HALO + lane, ZERO), inverse)
    rim = jnp.where(band < BANDS - 1, HALO + lane - 80, ZERO)
    inverse = jnp.where(jnp.logical_and(lane >= 80, lane < 96), rim, inverse)
    TBL[...] = jnp.zeros_like(TBL)
    TBL[0:1] = inverse
    TBL[1:2] = named
    to_smem = pltpu.make_async_copy(TBL, TBS, tbl_sem)
    to_smem.start()
    for t in order[3:]:
        first_out(t)

    def send_wind(dst):
        pltpu.make_async_remote_copy(
            src_ref=wind, dst_ref=WND.at[me], send_sem=wind_send, recv_sem=wind_recv,
            device_id=(band, dst), device_id_type=MESH,
        ).start()

    each_peer(send_wind)
    def rate_columns():
        for one in small_loads[7:]:
            one.wait()

        def columns(i, carry):
            part = pl.ds(pl.multiple_of(i * BLK, BLK), BLK)
            diag = lax.broadcasted_iota(jnp.int32, (BLK, BLK), 0) == lax.broadcasted_iota(jnp.int32, (BLK, BLK), 1)
            for src, dst in ((wr, WRB), (dis, DSB)):
                col = jnp.sum(jnp.where(diag, src[part].reshape(1, BLK), 0.0), axis=1, keepdims=True)
                dst[part, :] = jnp.broadcast_to(col, (BLK, BLK))
            return carry

        lax.fori_loop(0, K // BLK, columns, 0)
        rest = K % BLK
        diag = lax.broadcasted_iota(jnp.int32, (rest, rest), 0) == lax.broadcasted_iota(jnp.int32, (rest, rest), 1)
        for src, dst in ((wr, WRB), (dis, DSB)):
            col = jnp.sum(jnp.where(diag, src[K - rest:K].reshape(1, rest), 0.0), axis=1, keepdims=True)
            dst[K - rest:K, :] = jnp.broadcast_to(col, (rest, BLK))

    to_smem.wait()

    def neighbours(j, carry):
        q = TBS[1, j]
        place = lax.rem(q, 16)
        line = q - place + 16
        NB[0, j] = TBS[0, line + lax.rem(place + 15, 16)]
        NB[1, j] = TBS[0, line + lax.rem(place + 1, 16)]
        NB[2, j] = TBS[0, q]
        NB[3, j] = TBS[0, q + 32]
        return carry

    lax.fori_loop(0, SLOTS, neighbours, 0, unroll=8)

    wait_for(META.at[pl.ds(0, MEM - 1)], meta_recv)

    def line_at(found, r):
        got = found[0:1]
        for k in range(1, 4):
            got = jnp.where(r == k, found[k:k + 1], got)
        return got

    def place_meta(j, carry):
        q = TBS[1, j]
        place, r = lax.rem(q, 16), lax.div(q, 16)
        for layer in range(3):
            SM[j, layer:layer + 1] = line_at(META[place, layer], r)
        return carry

    lax.fori_loop(0, SLOTS, place_meta, 0, unroll=8)
    for one in table_loads:
        one.wait()

    lanes = lax.broadcasted_iota(jnp.int32, (TILE, BLK), 1)
    first_lane, last_lane = lanes == 0, lanes == BLK - 1

    def halo_copy(s, c, way):
        return pltpu.make_async_remote_copy(
            src_ref=HO.at[s, c, way], dst_ref=HI.at[s, c, way],
            send_sem=halo_send.at[s, c, way], recv_sem=halo_recv.at[s, c, way],
            device_id=(up if way == 0 else down, me), device_id_type=MESH,
        )

    def velocities(c):
        consts = C[c]
        aa, bb, cc, ss = (jnp.broadcast_to(consts[:, i:i + 1], (TILE, BLK)) for i in range(4))

        def one(j, carry):
            here = SM[j]
            speed = bb * jnp.tanh(aa * here[0:1])
            VX[c, j] = speed * cc + here[1:2]
            VY[c, j] = speed * ss + here[2:3]
            return carry

        lax.fori_loop(0, SLOTS, one, 0, unroll=8)

    def fluxes(s, c, par):
        if s == 0:
            velocities(c)
        wait_for(A.at[s, c, pl.ds(0, MEM - 1)], out_recv.at[s, c])

        def one(i, carry):
            for sl in range(2):
                j = 2 * i + sl
                g = A[s, c, i, sl].astype(F32)
                vx, vy = VX[c, j], VY[c, j]
                px, py = vx * g, vy * g
                east = jnp.where(vx > 0.0, px, 0.0)
                west = east - px
                north = jnp.where(vy > 0.0, py, 0.0)
                south = north - py
                from_west = pltpu.roll(east, 1, 1)
                from_east = pltpu.roll(west, BLK - 1, 1)
                inner = jnp.where(first_lane, 0.0, from_west) + jnp.where(last_lane, 0.0, from_east)
                NET[par, j] = inner - ((east + west) + (north + south))
                EDGE[par, j] = jnp.where(first_lane, from_west, from_east)
                FN[par, j] = north.astype(BF16)
                FS[par, j] = south.astype(BF16)
            return carry

        lax.fori_loop(0, MEM, one, 0, unroll=8)

        def edge(p, carry):
            HO[s, c, 0, p] = FN[par, TBS[0, 64 + p]]
            HO[s, c, 1, p] = FS[par, TBS[0, 16 + p]]
            return carry

        lax.fori_loop(0, MEM, edge, 0, unroll=4)
        halo_copy(s, c, 0).start()
        halo_copy(s, c, 1).start()

    def changes(s, c, par):
        halo_copy(s, c, 0).wait_recv()
        halo_copy(s, c, 1).wait_recv()
        FN[par, HALO:HALO + MEM] = HI[s, c, 0]
        FS[par, HALO:HALO + MEM] = HI[s, c, 1]

        def one(i, carry):
            for sl in range(2):
                j = 2 * i + sl
                sides = jnp.where(last_lane, EDGE[par, NB[1, j]], 0.0)
                sides = jnp.where(first_lane, EDGE[par, NB[0, j]], sides)
                lines = FN[par, NB[2, j]].astype(F32) + FS[par, NB[3, j]].astype(F32)
                R[s, c, i, sl] = (NET[par, j] + sides + lines).astype(BF16)
            return carry

        lax.fori_loop(0, MEM, one, 0, unroll=8)
        tile = 16 * c + me

        def send(dst):
            pltpu.make_async_remote_copy(
                src_ref=R.at[s, c, dst], dst_ref=D.at[s, tile],
                send_sem=ret_send.at[s, c], recv_sem=ret_recv.at[s, c],
                device_id=(band, dst), device_id_type=MESH,
            ).start()

        each_peer(send)
        D[s, tile] = R[s, c, me]

    def gather(s, r0, tiles, sums):
        def one(i, carry):
            rows = pl.ds(pl.multiple_of(r0 + i * TILE, TILE), TILE)
            new = []
            for sl in range(2):
                cols = slice(sl * BLK, (sl + 1) * BLK)
                x = S[rows, cols] + D[s, r0 // TILE + i, sl].astype(F32)
                S[rows, cols] = x
                LOW[rows, cols] = x.astype(BF16)
                new.append(carry[sl] + x * x)
            return tuple(new)

        return lax.fori_loop(0, tiles, one, sums, unroll=min(tiles, 4))

    def multiply(k0, depth, add, r0=0, height=432, parts=3):
        low = LOW[pl.ds(k0, depth), :]

        def one(i, carry):
            rows = pl.ds(pl.multiple_of(r0 + i * height, 16), height)
            for mix, total in ((M1, F1), (M2, F2)):
                got = jnp.dot(mix[rows, pl.ds(k0, depth)], low, preferred_element_type=F32)
                total[rows, :] = total[rows, :] + got if add else got
            return carry

        if parts == 1:
            one(0, 0)
        else:
            lax.fori_loop(0, parts, one, 0)

    def update(r0, tiles):
        def one(i, carry):
            rows = pl.ds(pl.multiple_of(r0 + i * TILE, TILE), TILE)
            for sl in range(2):
                x = sourced(S, F1, F2, WRB, DSB, OW, rows, sl)
                S[rows, sl * BLK:(sl + 1) * BLK] = x
                G[1, r0 // TILE + i, sl] = x.astype(BF16)
            return carry

        lax.fori_loop(0, tiles, one, 0, unroll=min(tiles, 4))

    start = jnp.where(me == HOT, -1, 0)
    for s in range(STEPS):
        def stage(i, carry, s=s):
            @pl.when(i < CHUNKS)
            def _():
                fluxes(s, jnp.where(i < 0, EXTRA, i), lax.rem(i + BUFS, BUFS))

            @pl.when(i > start + LAG - 1)
            def _():
                changes(s, jnp.where(i < LAG, EXTRA, i - LAG), lax.rem(i + BUFS - LAG, BUFS))

            return carry

        lax.fori_loop(start, CHUNKS + LAG, stage, 0)

        if s == 0:
            rate_columns()
            wait_for(WND.at[pl.ds(0, MEM - 1)], wind_recv)
            for sl in range(2):
                place, r = lax.rem(bl[sl], 16), lax.div(bl[sl], 16)
                cols = slice(sl * BLK, (sl + 1) * BLK)
                OW[0:1, cols] = jnp.where(line_at(META[place, 0], r) > 0.0, 1.0, 0.0)
                OW[1:2, cols] = 0.5 * line_at(WND[place], r)
            for one in mix_loads:
                one.wait()

        @pl.when(me != HOT)
        def _():
            wait_for(D.at[s, 80], ret_recv.at[s, EXTRA])

        zero = jnp.zeros((TILE, BLK), F32)
        sums = gather(s, 1280, 1, (zero, zero))
        multiply(1280, 16, False)

        def collect(t, sums, s=s):
            wait_for(D.at[s, pl.ds(16 * t, MEM - 1)], ret_recv.at[s, t])
            k0 = pl.multiple_of(t * 256, 256)
            sums = gather(s, k0, 16, sums)
            if s == 1 or t is not CHUNKS - 1:
                multiply(k0, 256, True)
            return sums

        if s == 0:
            sums = collect(CHUNKS - 1, lax.fori_loop(0, CHUNKS - 1, collect, sums))
        else:
            sums = lax.fori_loop(0, CHUNKS, collect, sums)
        for sl in range(2):
            mean = jnp.sum(sums[sl], axis=0, keepdims=True) * (1.0 / K)
            OW[2:3, sl * BLK:(sl + 1) * BLK] = 0.5 * jnp.sqrt(mean + 1e-06)

        if s == 0:
            multiply(1024, 256, True, 1280, 16, 1)
            update(1280, 1)
            send_out(1, EXTRA)

            def finish(t, carry):
                r0 = pl.multiple_of(t * 256, 256)
                multiply(1024, 256, True, r0, 256, 1)
                update(r0, 16)
                send_out(1, t)
                return carry

            lax.fori_loop(0, CHUNKS, finish, 0)

    wait_for(IDS.at[pl.ds(0, MEM - 1)], id_send)
    wait_for(META.at[pl.ds(0, MEM - 1)], meta_send)
    wait_for(WND.at[pl.ds(0, MEM - 1)], wind_send)
    for s in range(STEPS):
        wait_for(G.at[s, pl.ds(0, 75)], out_send.at[s, 0])

        @pl.when(me != HOT)
        def _():
            wait_for(G.at[s, 80], out_send.at[s, 1])

        @pl.when(me == HOT)
        def _():
            wait_for(R.at[s, EXTRA, pl.ds(0, MEM - 1)], ret_send.at[s, EXTRA])
            for way in range(2):
                halo_copy(s, EXTRA, way).wait_send()
        for t in range(CHUNKS):
            wait_for(R.at[s, t, pl.ds(0, MEM - 1)], ret_send.at[s, t])
            for way in range(2):
                halo_copy(s, t, way).wait_send()


def on_device(action, block_list, land_sea, ice, depth, cur_x, cur_y, wind, wind_rate, dissipation, mix1, mix2):
    hbm = pl.BlockSpec(memory_space=pltpu.HBM)
    dma = pltpu.SemaphoreType.DMA
    tile = (TILE, BLK)

    def pinned(x):
        return pltpu.with_memory_space_constraint(x, pltpu.HBM)

    state = pl.pallas_call(
        kernel,
        out_shape=[
            pltpu.VMEM((K, 256), F32),
            pltpu.VMEM((K, 256), F32),
            pltpu.VMEM((K, 256), F32),
            pltpu.VMEM((K, BLK), F32),
            pltpu.VMEM((K, BLK), F32),
            pltpu.VMEM((8, 256), F32),
        ],
        in_specs=[hbm] * 13,
        out_specs=[pl.BlockSpec(memory_space=pltpu.VMEM)] * 6,
        scratch_shapes=[
            pltpu.SMEM((4,), jnp.int32),
            pltpu.VMEM((4, BLK), jnp.int32),
            pltpu.VMEM((4, BLK), jnp.int32),
            pltpu.VMEM((4, BLK), F32),
            pltpu.VMEM((4, BLK), F32),
            pltpu.VMEM((4, BLK), F32),
            pltpu.VMEM((4, BLK), F32),
            pltpu.VMEM((K,), F32),
            pltpu.VMEM((K,), F32),
            pltpu.VMEM((K, K), BF16),
            pltpu.VMEM((K, K), BF16),
            pltpu.VMEM((K, 256), BF16),
            pltpu.VMEM((STEPS, TILES, 2) + tile, BF16),
            pltpu.VMEM((STEPS, 6, MEM, 2) + tile, BF16),
            pltpu.VMEM((STEPS, 6, MEM, 2) + tile, BF16),
            pltpu.VMEM((STEPS, TILES, 2) + tile, BF16),
            pltpu.VMEM((STEPS, 6, 2, MEM) + tile, BF16),
            pltpu.VMEM((STEPS, 6, 2, MEM) + tile, BF16),
            pltpu.VMEM((BUFS, SLOTS) + tile, F32),
            pltpu.VMEM((BUFS, SLOTS + 1) + tile, F32),
            pltpu.VMEM((BUFS, FIELD) + tile, BF16),
            pltpu.VMEM((BUFS, FIELD) + tile, BF16),
            pltpu.VMEM((6, SLOTS) + tile, F32),
            pltpu.VMEM((6, SLOTS) + tile, F32),
            pltpu.VMEM((SLOTS, 8, BLK), F32),
            pltpu.VMEM((3, 4, BLK), F32),
            pltpu.VMEM((MEM, 3, 4, BLK), F32),
            pltpu.VMEM((MEM, 4, BLK), F32),
            pltpu.VMEM((2, BLK), jnp.int32),
            pltpu.VMEM((MEM, 2, BLK), jnp.int32),
            pltpu.VMEM((8, BLK), jnp.int32),
            pltpu.SMEM((8, BLK), jnp.int32),
            pltpu.SMEM((4, SLOTS), jnp.int32),
            pltpu.VMEM((6,) + tile, F32),
            dma((9,)), dma((6,)), dma((2,)), dma((6,)), dma, dma, dma, dma, dma, dma, dma,
            dma((STEPS, 2)), dma((STEPS, 6)), dma((STEPS, 6, 2)), dma((STEPS, 6, 2)),
            dma((STEPS, 6)), dma((STEPS, 6)),
        ],
        compiler_params=pltpu.CompilerParams(
            collective_id=0, has_side_effects=True, vmem_limit_bytes=48 * 1024 * 1024
        ),
        cost_estimate=pl.CostEstimate(flops=7 * 10**9, bytes_accessed=10**7, transcendentals=10**6),
    )(
        *(
            pinned(x)
            for x in (
                block_list, land_sea, ice, depth, cur_x, cur_y, wind, wind_rate, dissipation,
                jnp.asarray(component_table()), action, mix1, mix2,
            )
        ),
    )
    return pl.pallas_call(
        last_kernel,
        out_shape=jax.ShapeDtypeStruct(action.shape, F32),
        in_specs=[pl.BlockSpec(memory_space=pltpu.VMEM)] * 6,
        out_specs=hbm,
        scratch_shapes=[
            pltpu.VMEM((K, 256), F32),
            pltpu.VMEM((K // 9, 256), F32),
            dma((9,)), dma((9,)),
        ],
        compiler_params=pltpu.CompilerParams(vmem_limit_bytes=8 * 1024 * 1024),
    )(*state)


def solution(mesh):
    col = P(None, ("band", "grp"))
    flat = P(("band", "grp"))
    grid = P("band", "grp")
    return jax.shard_map(
        on_device,
        mesh=mesh,
        in_specs=(col, flat, grid, grid, grid, grid, grid, grid, P(), P(), P(), P()),
        out_specs=col,
        check_vma=False,
    )
```

```python
import functools
import math

import jax
import jax.numpy as jnp
import numpy as np
from jax import lax
from jax.experimental import pallas as pl
from jax.experimental.pallas import tpu as pltpu
from jax.sharding import PartitionSpec as P

ND = 36
K = 1296
TILE = 16
TILES = 81
BLK = 128
MEM = 16
BANDS = 8
SLOTS = 32
STEPS = 2
CHUNKS = 5
EXTRA = 5
HOT = 0
LAG = 3
BUFS = LAG + 1
ORDER = sorted([(d // 4, d % 4) for d in range(1, 16)], key=lambda d: -min(d[0], 4 - d[0]) - min(d[1], 4 - d[1]))
ZERO = 32
HALO = 33
FIELD = 49
MESH = pl.DeviceIdType.MESH
F32 = jnp.float32
BF16 = jnp.bfloat16


def component_table():
    index = np.arange(K)
    freq = (index // ND).astype(np.float64)
    angle = 2.0 * math.pi * (index % ND) / ND
    table = np.zeros((K, BLK), np.float32)
    table[:, 0] = 1.0 + 0.25 * freq
    table[:, 1] = 0.4 * 0.93**freq
    table[:, 2] = np.cos(angle)
    table[:, 3] = np.sin(angle)
    return table.reshape(TILES, TILE, BLK)


def sourced(S, F1, F2, WRB, DSB, OW, rows, sl):
    cols = slice(sl * BLK, (sl + 1) * BLK)
    scale = 1.0 + (WRB[rows, :] * OW[1:2, cols] - DSB[rows, :] * OW[2:3, cols])
    gated = F1[rows, cols] * (0.25 + 0.25 * jnp.tanh(0.5 * F2[rows, cols]))
    return OW[0:1, cols] * (S[rows, cols] * scale + gated)


def last_kernel(S, F1, F2, WRB, DSB, OW, out, made, zeros, made_sem, zero_sem):
    zeros[...] = jnp.zeros_like(zeros)
    part = K // 9
    for n in range(9):
        pltpu.make_async_copy(
            zeros, out.at[pl.ds(part * n, part), pl.ds(256, 256)], zero_sem.at[n]
        ).start()

    def copy_of(n):
        rows = pl.ds(part * n, part)
        return pltpu.make_async_copy(made.at[rows], out.at[rows, pl.ds(0, 256)], made_sem.at[n])

    for n in range(9):
        def one(i, carry, n=n):
            rows = pl.ds(pl.multiple_of(part * n + i * TILE, TILE), TILE)
            for sl in range(2):
                made[rows, sl * BLK:(sl + 1) * BLK] = sourced(S, F1, F2, WRB, DSB, OW, rows, sl)
            return carry

        lax.fori_loop(0, part // TILE, one, 0, unroll=3)
        copy_of(n).start()
    for n in range(9):
        pltpu.make_async_copy(
            zeros, out.at[pl.ds(part * n, part), pl.ds(256, 256)], zero_sem.at[n]
        ).wait()
        copy_of(n).wait()


def kernel(
    bl_in, land_in, ice_in, depth_in, cur_x_in, cur_y_in, wind_in, wr_in, dis_in, cst, action, mix1, mix2,
    S, F1, F2, WRB, DSB, OW,
    bl, land, ice, depth, cur_x, cur_y, wind, wr, dis,
    M1, M2, LOW, G, A, R, D, HO, HI, NET, EDGE, FN, FS, VX, VY, SM,
    MT, META, WND, IDT, IDS, TBL, TBS, NB, C,
    small_sem, act_sem, mix_sem, cst_sem, tbl_sem, meta_send, meta_recv, id_send, id_recv, wind_send, wind_recv,
    out_send, out_recv, halo_send, halo_recv, ret_send, ret_recv,
):
    band = lax.axis_index("band")
    me = lax.axis_index("grp")
    up, down = lax.rem(band + 1, BANDS), lax.rem(band + BANDS - 1, BANDS)

    mx, my = lax.div(me, 4), lax.rem(me, 4)
    line_of = [4 * lax.rem(mx + d, 4) for d in range(4)]
    place_of = [lax.rem(my + d, 4) for d in range(4)]

    def each_peer(act):
        for dx, dy in ORDER:
            act(line_of[dx] + place_of[dy])

    def rows_of(t):
        return (1280, 16) if t == EXTRA else (256 * t, 256)

    order = [EXTRA] + list(range(CHUNKS))

    smalls = (
        (land_in, land), (ice_in, ice), (depth_in, depth), (cur_x_in, cur_x), (cur_y_in, cur_y),
        (wind_in, wind), (bl_in, bl), (wr_in, wr), (dis_in, dis),
    )
    small_loads = [pltpu.make_async_copy(a, c, small_sem.at[i]) for i, (a, c) in enumerate(smalls)]
    for one in small_loads:
        one.start()
    loads = {}
    for t in order:
        r0, n = rows_of(t)
        loads[t] = pltpu.make_async_copy(
            action.at[pl.ds(r0, n), pl.ds(0, 256)], S.at[pl.ds(r0, n)], act_sem.at[t]
        )
        loads[t].start()
    table_loads = []
    for t in range(CHUNKS + 1):
        tile = 80 if t == EXTRA else 16 * t + me
        table_loads.append(pltpu.make_async_copy(cst.at[tile], C.at[t], cst_sem.at[t]))
        table_loads[-1].start()
    mix_loads = [
        pltpu.make_async_copy(mix1, M1, mix_sem.at[0]),
        pltpu.make_async_copy(mix2, M2, mix_sem.at[1]),
    ]
    for one in mix_loads:
        one.start()

    barrier = pltpu.get_barrier_semaphore()

    def greet(dst):
        pl.semaphore_signal(barrier, inc=1, device_id=(band, dst), device_id_type=MESH)

    each_peer(greet)
    pl.semaphore_signal(barrier, inc=1, device_id=(up, me), device_id_type=MESH)
    pl.semaphore_signal(barrier, inc=1, device_id=(down, me), device_id_type=MESH)

    for one in small_loads[:7]:
        one.wait()
    wet = land[...].astype(F32) * (1.0 - ice[...].astype(F32))
    MT[0] = wet * depth[...]
    MT[1] = wet * cur_x[...]
    MT[2] = wet * cur_y[...]
    IDT[0:1] = jnp.full((1, BLK), bl[0], jnp.int32)
    IDT[1:2] = jnp.full((1, BLK), bl[1], jnp.int32)
    META[me] = MT[...]
    IDS[me] = IDT[...]
    WND[me] = wind[...]
    for ref in (EDGE, FN, FS):
        for par in range(BUFS):
            ref[par, ZERO] = jnp.zeros((TILE, BLK), ref.dtype)

    pl.semaphore_wait(barrier, MEM + 1)

    def send_meta(dst):
        pltpu.make_async_remote_copy(
            src_ref=IDT, dst_ref=IDS.at[me], send_sem=id_send, recv_sem=id_recv,
            device_id=(band, dst), device_id_type=MESH,
        ).start()
        pltpu.make_async_remote_copy(
            src_ref=MT, dst_ref=META.at[me], send_sem=meta_send, recv_sem=meta_recv,
            device_id=(band, dst), device_id_type=MESH,
        ).start()

    each_peer(send_meta)

    def send_out(s, t):
        if t is EXTRA:
            @pl.when(me != HOT)
            def _():
                pltpu.make_async_remote_copy(
                    src_ref=G.at[s, 80], dst_ref=A.at[s, EXTRA, me],
                    send_sem=out_send.at[s, 1], recv_sem=out_recv.at[s, EXTRA],
                    device_id=(band, HOT), device_id_type=MESH,
                ).start()

            @pl.when(me == HOT)
            def _():
                A[s, EXTRA, HOT] = G[s, 80]
            return

        def one(dst):
            pltpu.make_async_remote_copy(
                src_ref=G.at[s, 16 * t + dst], dst_ref=A.at[s, t, me],
                send_sem=out_send.at[s, 0], recv_sem=out_recv.at[s, t],
                device_id=(band, dst), device_id_type=MESH,
            ).start()

        each_peer(one)
        A[s, t, me] = G[s, 16 * t + me]

    def wait_for(ref, sem):
        pltpu.make_async_copy(ref, ref, sem).wait()

    def first_out(t):
        r0, n = rows_of(t)
        loads[t].wait()

        def pack(i, carry):
            rows = pl.ds(pl.multiple_of(r0 + i * TILE, TILE), TILE)
            for sl in range(2):
                G[0, r0 // TILE + i, sl] = S[rows, sl * BLK:(sl + 1) * BLK].astype(BF16)
            return carry

        lax.fori_loop(0, n // TILE, pack, 0, unroll=min(n // TILE, 4))
        send_out(0, t)

    for t in order[:3]:
        first_out(t)

    wait_for(IDS.at[pl.ds(0, MEM - 1)], id_recv)
    lane = lax.broadcasted_iota(jnp.int32, (1, BLK), 1)
    inverse = jnp.full((1, BLK), ZERO, jnp.int32)
    named = jnp.zeros((1, BLK), jnp.int32)
    for i in range(MEM):
        for sl in range(2):
            j = 2 * i + sl
            ident = IDS[i, sl:sl + 1, :]
            inverse = jnp.where(lane == ident + 16, j, inverse)
            named = jnp.where(lane == j, ident, named)
    inverse = jnp.where(lane < 16, jnp.where(band > 0, HALO + lane, ZERO), inverse)
    rim = jnp.where(band < BANDS - 1, HALO + lane - 80, ZERO)
    inverse = jnp.where(jnp.logical_and(lane >= 80, lane < 96), rim, inverse)
    TBL[...] = jnp.zeros_like(TBL)
    TBL[0:1] = inverse
    TBL[1:2] = named
    to_smem = pltpu.make_async_copy(TBL, TBS, tbl_sem)
    to_smem.start()
    for t in order[3:]:
        first_out(t)

    def send_wind(dst):
        pltpu.make_async_remote_copy(
            src_ref=wind, dst_ref=WND.at[me], send_sem=wind_send, recv_sem=wind_recv,
            device_id=(band, dst), device_id_type=MESH,
        ).start()

    each_peer(send_wind)
    def rate_columns():
        for one in small_loads[7:]:
            one.wait()

        def columns(i, carry):
            part = pl.ds(pl.multiple_of(i * BLK, BLK), BLK)
            diag = lax.broadcasted_iota(jnp.int32, (BLK, BLK), 0) == lax.broadcasted_iota(jnp.int32, (BLK, BLK), 1)
            for src, dst in ((wr, WRB), (dis, DSB)):
                col = jnp.sum(jnp.where(diag, src[part].reshape(1, BLK), 0.0), axis=1, keepdims=True)
                dst[part, :] = jnp.broadcast_to(col, (BLK, BLK))
            return carry

        lax.fori_loop(0, K // BLK, columns, 0)
        rest = K % BLK
        diag = lax.broadcasted_iota(jnp.int32, (rest, rest), 0) == lax.broadcasted_iota(jnp.int32, (rest, rest), 1)
        for src, dst in ((wr, WRB), (dis, DSB)):
            col = jnp.sum(jnp.where(diag, src[K - rest:K].reshape(1, rest), 0.0), axis=1, keepdims=True)
            dst[K - rest:K, :] = jnp.broadcast_to(col, (rest, BLK))

    to_smem.wait()

    def neighbours(j, carry):
        q = TBS[1, j]
        place = lax.rem(q, 16)
        line = q - place + 16
        NB[0, j] = TBS[0, line + lax.rem(place + 15, 16)]
        NB[1, j] = TBS[0, line + lax.rem(place + 1, 16)]
        NB[2, j] = TBS[0, q]
        NB[3, j] = TBS[0, q + 32]
        return carry

    lax.fori_loop(0, SLOTS, neighbours, 0, unroll=8)

    rate_columns()
    wait_for(META.at[pl.ds(0, MEM - 1)], meta_recv)

    def line_at(found, r):
        got = found[0:1]
        for k in range(1, 4):
            got = jnp.where(r == k, found[k:k + 1], got)
        return got

    def place_meta(j, carry):
        q = TBS[1, j]
        place, r = lax.rem(q, 16), lax.div(q, 16)
        for layer in range(3):
            SM[j, layer:layer + 1] = line_at(META[place, layer], r)
        return carry

    lax.fori_loop(0, SLOTS, place_meta, 0, unroll=8)
    for one in table_loads:
        one.wait()

    lanes = lax.broadcasted_iota(jnp.int32, (TILE, BLK), 1)
    first_lane, last_lane = lanes == 0, lanes == BLK - 1

    def halo_copy(s, c, way):
        return pltpu.make_async_remote_copy(
            src_ref=HO.at[s, c, way], dst_ref=HI.at[s, c, way],
            send_sem=halo_send.at[s, c, way], recv_sem=halo_recv.at[s, c, way],
            device_id=(up if way == 0 else down, me), device_id_type=MESH,
        )

    def velocities(c):
        consts = C[c]
        aa, bb, cc, ss = (jnp.broadcast_to(consts[:, i:i + 1], (TILE, BLK)) for i in range(4))

        def one(j, carry):
            here = SM[j]
            speed = bb * jnp.tanh(aa * here[0:1])
            VX[c, j] = speed * cc + here[1:2]
            VY[c, j] = speed * ss + here[2:3]
            return carry

        lax.fori_loop(0, SLOTS, one, 0, unroll=8)

    def fluxes(s, c, par):
        if s == 0:
            velocities(c)
        wait_for(A.at[s, c, pl.ds(0, MEM - 1)], out_recv.at[s, c])

        def one(i, carry):
            for sl in range(2):
                j = 2 * i + sl
                g = A[s, c, i, sl].astype(F32)
                vx, vy = VX[c, j], VY[c, j]
                px, py = vx * g, vy * g
                east = jnp.where(vx > 0.0, px, 0.0)
                west = east - px
                north = jnp.where(vy > 0.0, py, 0.0)
                south = north - py
                from_west = pltpu.roll(east, 1, 1)
                from_east = pltpu.roll(west, BLK - 1, 1)
                inner = jnp.where(first_lane, 0.0, from_west) + jnp.where(last_lane, 0.0, from_east)
                NET[par, j] = inner - ((east + west) + (north + south))
                EDGE[par, j] = jnp.where(first_lane, from_west, from_east)
                FN[par, j] = north.astype(BF16)
                FS[par, j] = south.astype(BF16)
            return carry

        lax.fori_loop(0, MEM, one, 0, unroll=8)

        def edge(p, carry):
            HO[s, c, 0, p] = FN[par, TBS[0, 64 + p]]
            HO[s, c, 1, p] = FS[par, TBS[0, 16 + p]]
            return carry

        lax.fori_loop(0, MEM, edge, 0, unroll=4)
        halo_copy(s, c, 0).start()
        halo_copy(s, c, 1).start()

    def changes(s, c, par):
        halo_copy(s, c, 0).wait_recv()
        halo_copy(s, c, 1).wait_recv()
        FN[par, HALO:HALO + MEM] = HI[s, c, 0]
        FS[par, HALO:HALO + MEM] = HI[s, c, 1]

        def one(i, carry):
            for sl in range(2):
                j = 2 * i + sl
                sides = jnp.where(last_lane, EDGE[par, NB[1, j]], 0.0)
                sides = jnp.where(first_lane, EDGE[par, NB[0, j]], sides)
                lines = FN[par, NB[2, j]].astype(F32) + FS[par, NB[3, j]].astype(F32)
                R[s, c, i, sl] = (NET[par, j] + sides + lines).astype(BF16)
            return carry

        lax.fori_loop(0, MEM, one, 0, unroll=8)
        tile = 16 * c + me

        def send(dst):
            pltpu.make_async_remote_copy(
                src_ref=R.at[s, c, dst], dst_ref=D.at[s, tile],
                send_sem=ret_send.at[s, c], recv_sem=ret_recv.at[s, c],
                device_id=(band, dst), device_id_type=MESH,
            ).start()

        each_peer(send)
        D[s, tile] = R[s, c, me]

    def gather(s, r0, tiles, sums):
        def one(i, carry):
            rows = pl.ds(pl.multiple_of(r0 + i * TILE, TILE), TILE)
            new = []
            for sl in range(2):
                cols = slice(sl * BLK, (sl + 1) * BLK)
                x = S[rows, cols] + D[s, r0 // TILE + i, sl].astype(F32)
                S[rows, cols] = x
                LOW[rows, cols] = x.astype(BF16)
                new.append(carry[sl] + x * x)
            return tuple(new)

        return lax.fori_loop(0, tiles, one, sums, unroll=min(tiles, 4))

    def multiply(k0, depth, add, r0=0, height=1296, parts=1):
        low = LOW[pl.ds(k0, depth), :]

        def one(i, carry):
            rows = pl.ds(pl.multiple_of(r0 + i * height, 16), height)
            for mix, total in ((M1, F1), (M2, F2)):
                got = jnp.dot(mix[rows, pl.ds(k0, depth)], low, preferred_element_type=F32)
                total[rows, :] = total[rows, :] + got if add else got
            return carry

        if parts == 1:
            one(0, 0)
        else:
            lax.fori_loop(0, parts, one, 0)

    def update(r0, tiles):
        def one(i, carry):
            rows = pl.ds(pl.multiple_of(r0 + i * TILE, TILE), TILE)
            for sl in range(2):
                x = sourced(S, F1, F2, WRB, DSB, OW, rows, sl)
                S[rows, sl * BLK:(sl + 1) * BLK] = x
                G[1, r0 // TILE + i, sl] = x.astype(BF16)
            return carry

        lax.fori_loop(0, tiles, one, 0, unroll=min(tiles, 4))

    start = jnp.where(me == HOT, -1, 0)
    for s in range(STEPS):
        def stage(i, carry, s=s):
            @pl.when(i < CHUNKS)
            def _():
                fluxes(s, jnp.where(i < 0, EXTRA, i), lax.rem(i + BUFS, BUFS))

            @pl.when(i > start + LAG - 1)
            def _():
                changes(s, jnp.where(i < LAG, EXTRA, i - LAG), lax.rem(i + BUFS - LAG, BUFS))

            return carry

        lax.fori_loop(start, CHUNKS + LAG, stage, 0)

        if s == 0:
            wait_for(WND.at[pl.ds(0, MEM - 1)], wind_recv)
            for sl in range(2):
                place, r = lax.rem(bl[sl], 16), lax.div(bl[sl], 16)
                cols = slice(sl * BLK, (sl + 1) * BLK)
                OW[0:1, cols] = jnp.where(line_at(META[place, 0], r) > 0.0, 1.0, 0.0)
                OW[1:2, cols] = 0.5 * line_at(WND[place], r)
            for one in mix_loads:
                one.wait()

        @pl.when(me != HOT)
        def _():
            wait_for(D.at[s, 80], ret_recv.at[s, EXTRA])

        zero = jnp.zeros((TILE, BLK), F32)
        sums = gather(s, 1280, 1, (zero, zero))
        multiply(1280, 16, False)

        def collect(t, sums, s=s):
            wait_for(D.at[s, pl.ds(16 * t, MEM - 1)], ret_recv.at[s, t])
            k0 = pl.multiple_of(t * 256, 256)
            sums = gather(s, k0, 16, sums)
            if s == 1 or t is not CHUNKS - 1:
                multiply(k0, 256, True)
            return sums

        if s == 0:
            sums = collect(CHUNKS - 1, lax.fori_loop(0, CHUNKS - 1, collect, sums))
        else:
            sums = lax.fori_loop(0, CHUNKS, collect, sums)
        for sl in range(2):
            mean = jnp.sum(sums[sl], axis=0, keepdims=True) * (1.0 / K)
            OW[2:3, sl * BLK:(sl + 1) * BLK] = 0.5 * jnp.sqrt(mean + 1e-06)

        if s == 0:
            multiply(1024, 256, True, 1280, 16, 1)
            update(1280, 1)
            send_out(1, EXTRA)

            def finish(t, carry):
                r0 = pl.multiple_of(t * 256, 256)
                multiply(1024, 256, True, r0, 256, 1)
                update(r0, 16)
                send_out(1, t)
                return carry

            lax.fori_loop(0, CHUNKS, finish, 0)

    wait_for(IDS.at[pl.ds(0, MEM - 1)], id_send)
    wait_for(META.at[pl.ds(0, MEM - 1)], meta_send)
    wait_for(WND.at[pl.ds(0, MEM - 1)], wind_send)
    for s in range(STEPS):
        wait_for(G.at[s, pl.ds(0, 75)], out_send.at[s, 0])

        @pl.when(me != HOT)
        def _():
            wait_for(G.at[s, 80], out_send.at[s, 1])

        @pl.when(me == HOT)
        def _():
            wait_for(R.at[s, EXTRA, pl.ds(0, MEM - 1)], ret_send.at[s, EXTRA])
            for way in range(2):
                halo_copy(s, EXTRA, way).wait_send()
        for t in range(CHUNKS):
            wait_for(R.at[s, t, pl.ds(0, MEM - 1)], ret_send.at[s, t])
            for way in range(2):
                halo_copy(s, t, way).wait_send()


def on_device(action, block_list, land_sea, ice, depth, cur_x, cur_y, wind, wind_rate, dissipation, mix1, mix2):
    hbm = pl.BlockSpec(memory_space=pltpu.HBM)
    dma = pltpu.SemaphoreType.DMA
    tile = (TILE, BLK)

    def pinned(x):
        return pltpu.with_memory_space_constraint(x, pltpu.HBM)

    state = pl.pallas_call(
        kernel,
        out_shape=[
            pltpu.VMEM((K, 256), F32),
            pltpu.VMEM((K, 256), F32),
            pltpu.VMEM((K, 256), F32),
            pltpu.VMEM((K, BLK), F32),
            pltpu.VMEM((K, BLK), F32),
            pltpu.VMEM((8, 256), F32),
        ],
        in_specs=[hbm] * 13,
        out_specs=[pl.BlockSpec(memory_space=pltpu.VMEM)] * 6,
        scratch_shapes=[
            pltpu.SMEM((4,), jnp.int32),
            pltpu.VMEM((4, BLK), jnp.int32),
            pltpu.VMEM((4, BLK), jnp.int32),
            pltpu.VMEM((4, BLK), F32),
            pltpu.VMEM((4, BLK), F32),
            pltpu.VMEM((4, BLK), F32),
            pltpu.VMEM((4, BLK), F32),
            pltpu.VMEM((K,), F32),
            pltpu.VMEM((K,), F32),
            pltpu.VMEM((K, K), BF16),
            pltpu.VMEM((K, K), BF16),
            pltpu.VMEM((K, 256), BF16),
            pltpu.VMEM((STEPS, TILES, 2) + tile, BF16),
            pltpu.VMEM((STEPS, 6, MEM, 2) + tile, BF16),
            pltpu.VMEM((STEPS, 6, MEM, 2) + tile, BF16),
            pltpu.VMEM((STEPS, TILES, 2) + tile, BF16),
            pltpu.VMEM((STEPS, 6, 2, MEM) + tile, BF16),
            pltpu.VMEM((STEPS, 6, 2, MEM) + tile, BF16),
            pltpu.VMEM((BUFS, SLOTS) + tile, F32),
            pltpu.VMEM((BUFS, SLOTS + 1) + tile, F32),
            pltpu.VMEM((BUFS, FIELD) + tile, BF16),
            pltpu.VMEM((BUFS, FIELD) + tile, BF16),
            pltpu.VMEM((6, SLOTS) + tile, F32),
            pltpu.VMEM((6, SLOTS) + tile, F32),
            pltpu.VMEM((SLOTS, 8, BLK), F32),
            pltpu.VMEM((3, 4, BLK), F32),
            pltpu.VMEM((MEM, 3, 4, BLK), F32),
            pltpu.VMEM((MEM, 4, BLK), F32),
            pltpu.VMEM((2, BLK), jnp.int32),
            pltpu.VMEM((MEM, 2, BLK), jnp.int32),
            pltpu.VMEM((8, BLK), jnp.int32),
            pltpu.SMEM((8, BLK), jnp.int32),
            pltpu.SMEM((4, SLOTS), jnp.int32),
            pltpu.VMEM((6,) + tile, F32),
            dma((9,)), dma((6,)), dma((2,)), dma((6,)), dma, dma, dma, dma, dma, dma, dma,
            dma((STEPS, 2)), dma((STEPS, 6)), dma((STEPS, 6, 2)), dma((STEPS, 6, 2)),
            dma((STEPS, 6)), dma((STEPS, 6)),
        ],
        compiler_params=pltpu.CompilerParams(
            collective_id=0, has_side_effects=True, vmem_limit_bytes=48 * 1024 * 1024
        ),
        cost_estimate=pl.CostEstimate(flops=7 * 10**9, bytes_accessed=10**7, transcendentals=10**6),
    )(
        *(
            pinned(x)
            for x in (
                block_list, land_sea, ice, depth, cur_x, cur_y, wind, wind_rate, dissipation,
                jnp.asarray(component_table()), action, mix1, mix2,
            )
        ),
    )
    return pl.pallas_call(
        last_kernel,
        out_shape=jax.ShapeDtypeStruct(action.shape, F32),
        in_specs=[pl.BlockSpec(memory_space=pltpu.VMEM)] * 6,
        out_specs=hbm,
        scratch_shapes=[
            pltpu.VMEM((K, 256), F32),
            pltpu.VMEM((K // 9, 256), F32),
            dma((9,)), dma((9,)),
        ],
        compiler_params=pltpu.CompilerParams(vmem_limit_bytes=8 * 1024 * 1024),
    )(*state)


def solution(mesh):
    col = P(None, ("band", "grp"))
    flat = P(("band", "grp"))
    grid = P("band", "grp")
    return jax.shard_map(
        on_device,
        mesh=mesh,
        in_specs=(col, flat, grid, grid, grid, grid, grid, grid, P(), P(), P(), P()),
        out_specs=col,
        check_vma=False,
    )
```

```python
import functools
import math

import jax
import jax.numpy as jnp
import numpy as np
from jax import lax
from jax.experimental import pallas as pl
from jax.experimental.pallas import tpu as pltpu
from jax.sharding import PartitionSpec as P

ND = 36
K = 1296
TILE = 16
TILES = 81
BLK = 128
MEM = 16
BANDS = 8
SLOTS = 32
STEPS = 2
CHUNKS = 5
EXTRA = 5
LAG = 3
BUFS = LAG + 1
ORDER = sorted([(d // 4, d % 4) for d in range(1, 16)], key=lambda d: -min(d[0], 4 - d[0]) - min(d[1], 4 - d[1]))
ZERO = 32
HALO = 33
FIELD = 49
MESH = pl.DeviceIdType.MESH
F32 = jnp.float32
BF16 = jnp.bfloat16


def component_table():
    index = np.arange(K)
    freq = (index // ND).astype(np.float64)
    angle = 2.0 * math.pi * (index % ND) / ND
    table = np.zeros((K, BLK), np.float32)
    table[:, 0] = 1.0 + 0.25 * freq
    table[:, 1] = 0.4 * 0.93**freq
    table[:, 2] = np.cos(angle)
    table[:, 3] = np.sin(angle)
    return table.reshape(TILES, TILE, BLK)


def sourced(S, F1, F2, WRB, DSB, OW, rows, sl):
    cols = slice(sl * BLK, (sl + 1) * BLK)
    scale = 1.0 + (WRB[rows, :] * OW[1:2, cols] - DSB[rows, :] * OW[2:3, cols])
    gated = F1[rows, cols] * (0.25 + 0.25 * jnp.tanh(0.5 * F2[rows, cols]))
    return OW[0:1, cols] * (S[rows, cols] * scale + gated)


def last_kernel(S, F1, F2, WRB, DSB, OW, out, made, zeros, made_sem, zero_sem):
    zeros[...] = jnp.zeros_like(zeros)
    part = K // 9
    for n in range(9):
        pltpu.make_async_copy(
            zeros, out.at[pl.ds(part * n, part), pl.ds(256, 256)], zero_sem.at[n]
        ).start()

    def copy_of(n):
        rows = pl.ds(part * n, part)
        return pltpu.make_async_copy(made.at[rows], out.at[rows, pl.ds(0, 256)], made_sem.at[n])

    for n in range(9):
        def one(i, carry, n=n):
            rows = pl.ds(pl.multiple_of(part * n + i * TILE, TILE), TILE)
            for sl in range(2):
                made[rows, sl * BLK:(sl + 1) * BLK] = sourced(S, F1, F2, WRB, DSB, OW, rows, sl)
            return carry

        lax.fori_loop(0, part // TILE, one, 0, unroll=3)
        copy_of(n).start()
    for n in range(9):
        pltpu.make_async_copy(
            zeros, out.at[pl.ds(part * n, part), pl.ds(256, 256)], zero_sem.at[n]
        ).wait()
        copy_of(n).wait()


def kernel(
    bl_in, land_in, ice_in, depth_in, cur_x_in, cur_y_in, wind_in, wr_in, dis_in, cst, action, mix1, mix2,
    S, F1, F2, WRB, DSB, OW,
    bl, land, ice, depth, cur_x, cur_y, wind, wr, dis,
    M1, M2, LOW, G, A, R, D, HO, HI, NET, EDGE, FN, FS, VX, VY, SM,
    MT, META, WND, IDT, IDS, TBL, TBS, NB, C,
    small_sem, act_sem, mix_sem, cst_sem, tbl_sem, meta_send, meta_recv, id_send, id_recv, wind_send, wind_recv,
    out_send, out_recv, halo_send, halo_recv, ret_send, ret_recv,
):
    band = lax.axis_index("band")
    me = lax.axis_index("grp")
    up, down = lax.rem(band + 1, BANDS), lax.rem(band + BANDS - 1, BANDS)

    hot = 10 * lax.rem(band, 2)
    hot_beside = 10 - hot
    mx, my = lax.div(me, 4), lax.rem(me, 4)
    line_of = [4 * lax.rem(mx + d, 4) for d in range(4)]
    place_of = [lax.rem(my + d, 4) for d in range(4)]

    def each_peer(act):
        for dx, dy in ORDER:
            act(line_of[dx] + place_of[dy])

    def rows_of(t):
        return (1280, 16) if t == EXTRA else (256 * t, 256)

    order = [EXTRA] + list(range(CHUNKS))

    smalls = (
        (land_in, land), (ice_in, ice), (depth_in, depth), (cur_x_in, cur_x), (cur_y_in, cur_y),
        (wind_in, wind), (bl_in, bl), (wr_in, wr), (dis_in, dis),
    )
    small_loads = [pltpu.make_async_copy(a, c, small_sem.at[i]) for i, (a, c) in enumerate(smalls)]
    for one in small_loads:
        one.start()
    loads = {}
    for t in order:
        r0, n = rows_of(t)
        loads[t] = pltpu.make_async_copy(
            action.at[pl.ds(r0, n), pl.ds(0, 256)], S.at[pl.ds(r0, n)], act_sem.at[t]
        )
        loads[t].start()
    table_loads = []
    for t in range(CHUNKS + 1):
        tile = 80 if t == EXTRA else 16 * t + me
        table_loads.append(pltpu.make_async_copy(cst.at[tile], C.at[t], cst_sem.at[t]))
        table_loads[-1].start()
    mix_loads = [
        pltpu.make_async_copy(mix1, M1, mix_sem.at[0]),
        pltpu.make_async_copy(mix2, M2, mix_sem.at[1]),
    ]
    for one in mix_loads:
        one.start()

    barrier = pltpu.get_barrier_semaphore()

    def greet(dst):
        pl.semaphore_signal(barrier, inc=1, device_id=(band, dst), device_id_type=MESH)

    each_peer(greet)
    pl.semaphore_signal(barrier, inc=1, device_id=(up, me), device_id_type=MESH)
    pl.semaphore_signal(barrier, inc=1, device_id=(down, me), device_id_type=MESH)

    @pl.when(me == hot)
    def _():
        for side in (up, down):
            pl.semaphore_signal(barrier, inc=1, device_id=(side, hot_beside), device_id_type=MESH)

    for one in small_loads[:7]:
        one.wait()
    wet = land[...].astype(F32) * (1.0 - ice[...].astype(F32))
    MT[0] = wet * depth[...]
    MT[1] = wet * cur_x[...]
    MT[2] = wet * cur_y[...]
    IDT[0:1] = jnp.full((1, BLK), bl[0], jnp.int32)
    IDT[1:2] = jnp.full((1, BLK), bl[1], jnp.int32)
    META[me] = MT[...]
    IDS[me] = IDT[...]
    WND[me] = wind[...]
    for ref in (EDGE, FN, FS):
        for par in range(BUFS):
            ref[par, ZERO] = jnp.zeros((TILE, BLK), ref.dtype)

    pl.semaphore_wait(barrier, MEM + 1 + jnp.where(me == hot, 2, 0))

    def send_meta(dst):
        pltpu.make_async_remote_copy(
            src_ref=IDT, dst_ref=IDS.at[me], send_sem=id_send, recv_sem=id_recv,
            device_id=(band, dst), device_id_type=MESH,
        ).start()
        pltpu.make_async_remote_copy(
            src_ref=MT, dst_ref=META.at[me], send_sem=meta_send, recv_sem=meta_recv,
            device_id=(band, dst), device_id_type=MESH,
        ).start()

    each_peer(send_meta)

    def send_out(s, t):
        if t is EXTRA:
            @pl.when(me != hot)
            def _():
                pltpu.make_async_remote_copy(
                    src_ref=G.at[s, 80], dst_ref=A.at[s, EXTRA, me],
                    send_sem=out_send.at[s, 1], recv_sem=out_recv.at[s, EXTRA],
                    device_id=(band, hot), device_id_type=MESH,
                ).start()

            @pl.when(me == hot)
            def _():
                A[s, EXTRA, me] = G[s, 80]
            return

        def one(dst):
            pltpu.make_async_remote_copy(
                src_ref=G.at[s, 16 * t + dst], dst_ref=A.at[s, t, me],
                send_sem=out_send.at[s, 0], recv_sem=out_recv.at[s, t],
                device_id=(band, dst), device_id_type=MESH,
            ).start()

        each_peer(one)
        A[s, t, me] = G[s, 16 * t + me]

    def wait_for(ref, sem):
        pltpu.make_async_copy(ref, ref, sem).wait()

    def first_out(t):
        r0, n = rows_of(t)
        loads[t].wait()

        def pack(i, carry):
            rows = pl.ds(pl.multiple_of(r0 + i * TILE, TILE), TILE)
            for sl in range(2):
                G[0, r0 // TILE + i, sl] = S[rows, sl * BLK:(sl + 1) * BLK].astype(BF16)
            return carry

        lax.fori_loop(0, n // TILE, pack, 0, unroll=min(n // TILE, 4))
        send_out(0, t)

    for t in order[:3]:
        first_out(t)

    wait_for(IDS.at[pl.ds(0, MEM - 1)], id_recv)
    lane = lax.broadcasted_iota(jnp.int32, (1, BLK), 1)
    inverse = jnp.full((1, BLK), ZERO, jnp.int32)
    named = jnp.zeros((1, BLK), jnp.int32)
    for i in range(MEM):
        for sl in range(2):
            j = 2 * i + sl
            ident = IDS[i, sl:sl + 1, :]
            inverse = jnp.where(lane == ident + 16, j, inverse)
            named = jnp.where(lane == j, ident, named)
    inverse = jnp.where(lane < 16, jnp.where(band > 0, HALO + lane, ZERO), inverse)
    rim = jnp.where(band < BANDS - 1, HALO + lane - 80, ZERO)
    inverse = jnp.where(jnp.logical_and(lane >= 80, lane < 96), rim, inverse)
    TBL[...] = jnp.zeros_like(TBL)
    TBL[0:1] = inverse
    TBL[1:2] = named
    to_smem = pltpu.make_async_copy(TBL, TBS, tbl_sem)
    to_smem.start()
    for t in order[3:]:
        first_out(t)

    def send_wind(dst):
        pltpu.make_async_remote_copy(
            src_ref=wind, dst_ref=WND.at[me], send_sem=wind_send, recv_sem=wind_recv,
            device_id=(band, dst), device_id_type=MESH,
        ).start()

    each_peer(send_wind)
    def rate_columns():
        for one in small_loads[7:]:
            one.wait()

        def columns(i, carry):
            part = pl.ds(pl.multiple_of(i * BLK, BLK), BLK)
            diag = lax.broadcasted_iota(jnp.int32, (BLK, BLK), 0) == lax.broadcasted_iota(jnp.int32, (BLK, BLK), 1)
            for src, dst in ((wr, WRB), (dis, DSB)):
                col = jnp.sum(jnp.where(diag, src[part].reshape(1, BLK), 0.0), axis=1, keepdims=True)
                dst[part, :] = jnp.broadcast_to(col, (BLK, BLK))
            return carry

        lax.fori_loop(0, K // BLK, columns, 0)
        rest = K % BLK
        diag = lax.broadcasted_iota(jnp.int32, (rest, rest), 0) == lax.broadcasted_iota(jnp.int32, (rest, rest), 1)
        for src, dst in ((wr, WRB), (dis, DSB)):
            col = jnp.sum(jnp.where(diag, src[K - rest:K].reshape(1, rest), 0.0), axis=1, keepdims=True)
            dst[K - rest:K, :] = jnp.broadcast_to(col, (rest, BLK))

    to_smem.wait()

    def neighbours(j, carry):
        q = TBS[1, j]
        place = lax.rem(q, 16)
        line = q - place + 16
        NB[0, j] = TBS[0, line + lax.rem(place + 15, 16)]
        NB[1, j] = TBS[0, line + lax.rem(place + 1, 16)]
        NB[2, j] = TBS[0, q]
        NB[3, j] = TBS[0, q + 32]
        return carry

    lax.fori_loop(0, SLOTS, neighbours, 0, unroll=8)

    rate_columns()
    wait_for(META.at[pl.ds(0, MEM - 1)], meta_recv)

    def line_at(found, r):
        got = found[0:1]
        for k in range(1, 4):
            got = jnp.where(r == k, found[k:k + 1], got)
        return got

    def place_meta(j, carry):
        q = TBS[1, j]
        place, r = lax.rem(q, 16), lax.div(q, 16)
        for layer in range(3):
            SM[j, layer:layer + 1] = line_at(META[place, layer], r)
        return carry

    lax.fori_loop(0, SLOTS, place_meta, 0, unroll=8)
    for one in table_loads:
        one.wait()

    lanes = lax.broadcasted_iota(jnp.int32, (TILE, BLK), 1)
    first_lane, last_lane = lanes == 0, lanes == BLK - 1

    def halo_copy(s, c, way):
        return pltpu.make_async_remote_copy(
            src_ref=HO.at[s, c, way], dst_ref=HI.at[s, c, way],
            send_sem=halo_send.at[s, c, way], recv_sem=halo_recv.at[s, c, way],
            device_id=(up if way == 0 else down, jnp.where(c == EXTRA, hot_beside, me)), device_id_type=MESH,
        )

    def velocities(c):
        consts = C[c]
        aa, bb, cc, ss = (jnp.broadcast_to(consts[:, i:i + 1], (TILE, BLK)) for i in range(4))

        def one(j, carry):
            here = SM[j]
            speed = bb * jnp.tanh(aa * here[0:1])
            VX[c, j] = speed * cc + here[1:2]
            VY[c, j] = speed * ss + here[2:3]
            return carry

        lax.fori_loop(0, SLOTS, one, 0, unroll=8)

    def fluxes(s, c, par):
        if s == 0:
            velocities(c)
        wait_for(A.at[s, c, pl.ds(0, MEM - 1)], out_recv.at[s, c])

        def one(i, carry):
            for sl in range(2):
                j = 2 * i + sl
                g = A[s, c, i, sl].astype(F32)
                vx, vy = VX[c, j], VY[c, j]
                px, py = vx * g, vy * g
                east = jnp.where(vx > 0.0, px, 0.0)
                west = east - px
                north = jnp.where(vy > 0.0, py, 0.0)
                south = north - py
                from_west = pltpu.roll(east, 1, 1)
                from_east = pltpu.roll(west, BLK - 1, 1)
                inner = jnp.where(first_lane, 0.0, from_west) + jnp.where(last_lane, 0.0, from_east)
                NET[par, j] = inner - ((east + west) + (north + south))
                EDGE[par, j] = jnp.where(first_lane, from_west, from_east)
                FN[par, j] = north.astype(BF16)
                FS[par, j] = south.astype(BF16)
            return carry

        lax.fori_loop(0, MEM, one, 0, unroll=8)

        def edge(p, carry):
            HO[s, c, 0, p] = FN[par, TBS[0, 64 + p]]
            HO[s, c, 1, p] = FS[par, TBS[0, 16 + p]]
            return carry

        lax.fori_loop(0, MEM, edge, 0, unroll=4)
        halo_copy(s, c, 0).start()
        halo_copy(s, c, 1).start()

    def changes(s, c, par):
        halo_copy(s, c, 0).wait_recv()
        halo_copy(s, c, 1).wait_recv()
        FN[par, HALO:HALO + MEM] = HI[s, c, 0]
        FS[par, HALO:HALO + MEM] = HI[s, c, 1]

        def one(i, carry):
            for sl in range(2):
                j = 2 * i + sl
                sides = jnp.where(last_lane, EDGE[par, NB[1, j]], 0.0)
                sides = jnp.where(first_lane, EDGE[par, NB[0, j]], sides)
                lines = FN[par, NB[2, j]].astype(F32) + FS[par, NB[3, j]].astype(F32)
                R[s, c, i, sl] = (NET[par, j] + sides + lines).astype(BF16)
            return carry

        lax.fori_loop(0, MEM, one, 0, unroll=8)
        tile = jnp.where(c == EXTRA, 80, 16 * c + me)

        def send(dst):
            pltpu.make_async_remote_copy(
                src_ref=R.at[s, c, dst], dst_ref=D.at[s, tile],
                send_sem=ret_send.at[s, c], recv_sem=ret_recv.at[s, c],
                device_id=(band, dst), device_id_type=MESH,
            ).start()

        each_peer(send)
        D[s, tile] = R[s, c, me]

    def gather(s, r0, tiles, sums):
        def one(i, carry):
            rows = pl.ds(pl.multiple_of(r0 + i * TILE, TILE), TILE)
            new = []
            for sl in range(2):
                cols = slice(sl * BLK, (sl + 1) * BLK)
                x = S[rows, cols] + D[s, r0 // TILE + i, sl].astype(F32)
                S[rows, cols] = x
                LOW[rows, cols] = x.astype(BF16)
                new.append(carry[sl] + x * x)
            return tuple(new)

        return lax.fori_loop(0, tiles, one, sums, unroll=min(tiles, 4))

    def multiply(k0, depth, add, r0=0, height=1296, parts=1):
        low = LOW[pl.ds(k0, depth), :]

        def one(i, carry):
            rows = pl.ds(pl.multiple_of(r0 + i * height, 16), height)
            for mix, total in ((M1, F1), (M2, F2)):
                got = jnp.dot(mix[rows, pl.ds(k0, depth)], low, preferred_element_type=F32)
                total[rows, :] = total[rows, :] + got if add else got
            return carry

        if parts == 1:
            one(0, 0)
        else:
            lax.fori_loop(0, parts, one, 0)

    def update(r0, tiles):
        def one(i, carry):
            rows = pl.ds(pl.multiple_of(r0 + i * TILE, TILE), TILE)
            for sl in range(2):
                x = sourced(S, F1, F2, WRB, DSB, OW, rows, sl)
                S[rows, sl * BLK:(sl + 1) * BLK] = x
                G[1, r0 // TILE + i, sl] = x.astype(BF16)
            return carry

        lax.fori_loop(0, tiles, one, 0, unroll=min(tiles, 4))

    start = jnp.where(me == hot, -1, 0)
    for s in range(STEPS):
        def stage(i, carry, s=s):
            @pl.when(i < CHUNKS)
            def _():
                fluxes(s, jnp.where(i < 0, EXTRA, i), lax.rem(i + BUFS, BUFS))

            @pl.when(i > start + LAG - 1)
            def _():
                changes(s, jnp.where(i < LAG, EXTRA, i - LAG), lax.rem(i + BUFS - LAG, BUFS))

            return carry

        lax.fori_loop(start, CHUNKS + LAG, stage, 0)

        if s == 0:
            wait_for(WND.at[pl.ds(0, MEM - 1)], wind_recv)
            for sl in range(2):
                place, r = lax.rem(bl[sl], 16), lax.div(bl[sl], 16)
                cols = slice(sl * BLK, (sl + 1) * BLK)
                OW[0:1, cols] = jnp.where(line_at(META[place, 0], r) > 0.0, 1.0, 0.0)
                OW[1:2, cols] = 0.5 * line_at(WND[place], r)
            for one in mix_loads:
                one.wait()

        @pl.when(me != hot)
        def _():
            wait_for(D.at[s, 80], ret_recv.at[s, EXTRA])

        zero = jnp.zeros((TILE, BLK), F32)
        sums = gather(s, 1280, 1, (zero, zero))
        multiply(1280, 16, False)

        def collect(t, sums, s=s):
            wait_for(D.at[s, pl.ds(16 * t, MEM - 1)], ret_recv.at[s, t])
            k0 = pl.multiple_of(t * 256, 256)
            sums = gather(s, k0, 16, sums)
            if s == 1 or t is not CHUNKS - 1:
                multiply(k0, 256, True)
            return sums

        if s == 0:
            sums = collect(CHUNKS - 1, lax.fori_loop(0, CHUNKS - 1, collect, sums))
        else:
            sums = lax.fori_loop(0, CHUNKS, collect, sums)
        for sl in range(2):
            mean = jnp.sum(sums[sl], axis=0, keepdims=True) * (1.0 / K)
            OW[2:3, sl * BLK:(sl + 1) * BLK] = 0.5 * jnp.sqrt(mean + 1e-06)

        if s == 0:
            multiply(1024, 256, True, 1280, 16, 1)
            update(1280, 1)
            send_out(1, EXTRA)

            def finish(t, carry):
                r0 = pl.multiple_of(t * 256, 256)
                multiply(1024, 256, True, r0, 256, 1)
                update(r0, 16)
                send_out(1, t)
                return carry

            lax.fori_loop(0, CHUNKS, finish, 0)

    wait_for(IDS.at[pl.ds(0, MEM - 1)], id_send)
    wait_for(META.at[pl.ds(0, MEM - 1)], meta_send)
    wait_for(WND.at[pl.ds(0, MEM - 1)], wind_send)
    for s in range(STEPS):
        wait_for(G.at[s, pl.ds(0, 75)], out_send.at[s, 0])

        @pl.when(me != hot)
        def _():
            wait_for(G.at[s, 80], out_send.at[s, 1])

        @pl.when(me == hot)
        def _():
            wait_for(R.at[s, EXTRA, pl.ds(0, MEM - 1)], ret_send.at[s, EXTRA])
            for way in range(2):
                halo_copy(s, EXTRA, way).wait_send()
        for t in range(CHUNKS):
            wait_for(R.at[s, t, pl.ds(0, MEM - 1)], ret_send.at[s, t])
            for way in range(2):
                halo_copy(s, t, way).wait_send()


def on_device(action, block_list, land_sea, ice, depth, cur_x, cur_y, wind, wind_rate, dissipation, mix1, mix2):
    hbm = pl.BlockSpec(memory_space=pltpu.HBM)
    dma = pltpu.SemaphoreType.DMA
    tile = (TILE, BLK)

    def pinned(x):
        return pltpu.with_memory_space_constraint(x, pltpu.HBM)

    state = pl.pallas_call(
        kernel,
        out_shape=[
            pltpu.VMEM((K, 256), F32),
            pltpu.VMEM((K, 256), F32),
            pltpu.VMEM((K, 256), F32),
            pltpu.VMEM((K, BLK), F32),
            pltpu.VMEM((K, BLK), F32),
            pltpu.VMEM((8, 256), F32),
        ],
        in_specs=[hbm] * 13,
        out_specs=[pl.BlockSpec(memory_space=pltpu.VMEM)] * 6,
        scratch_shapes=[
            pltpu.SMEM((4,), jnp.int32),
            pltpu.VMEM((4, BLK), jnp.int32),
            pltpu.VMEM((4, BLK), jnp.int32),
            pltpu.VMEM((4, BLK), F32),
            pltpu.VMEM((4, BLK), F32),
            pltpu.VMEM((4, BLK), F32),
            pltpu.VMEM((4, BLK), F32),
            pltpu.VMEM((K,), F32),
            pltpu.VMEM((K,), F32),
            pltpu.VMEM((K, K), BF16),
            pltpu.VMEM((K, K), BF16),
            pltpu.VMEM((K, 256), BF16),
            pltpu.VMEM((STEPS, TILES, 2) + tile, BF16),
            pltpu.VMEM((STEPS, 6, MEM, 2) + tile, BF16),
            pltpu.VMEM((STEPS, 6, MEM, 2) + tile, BF16),
            pltpu.VMEM((STEPS, TILES, 2) + tile, BF16),
            pltpu.VMEM((STEPS, 6, 2, MEM) + tile, BF16),
            pltpu.VMEM((STEPS, 6, 2, MEM) + tile, BF16),
            pltpu.VMEM((BUFS, SLOTS) + tile, F32),
            pltpu.VMEM((BUFS, SLOTS + 1) + tile, F32),
            pltpu.VMEM((BUFS, FIELD) + tile, BF16),
            pltpu.VMEM((BUFS, FIELD) + tile, BF16),
            pltpu.VMEM((6, SLOTS) + tile, F32),
            pltpu.VMEM((6, SLOTS) + tile, F32),
            pltpu.VMEM((SLOTS, 8, BLK), F32),
            pltpu.VMEM((3, 4, BLK), F32),
            pltpu.VMEM((MEM, 3, 4, BLK), F32),
            pltpu.VMEM((MEM, 4, BLK), F32),
            pltpu.VMEM((2, BLK), jnp.int32),
            pltpu.VMEM((MEM, 2, BLK), jnp.int32),
            pltpu.VMEM((8, BLK), jnp.int32),
            pltpu.SMEM((8, BLK), jnp.int32),
            pltpu.SMEM((4, SLOTS), jnp.int32),
            pltpu.VMEM((6,) + tile, F32),
            dma((9,)), dma((6,)), dma((2,)), dma((6,)), dma, dma, dma, dma, dma, dma, dma,
            dma((STEPS, 2)), dma((STEPS, 6)), dma((STEPS, 6, 2)), dma((STEPS, 6, 2)),
            dma((STEPS, 6)), dma((STEPS, 6)),
        ],
        compiler_params=pltpu.CompilerParams(
            collective_id=0, has_side_effects=True, vmem_limit_bytes=48 * 1024 * 1024
        ),
        cost_estimate=pl.CostEstimate(flops=7 * 10**9, bytes_accessed=10**7, transcendentals=10**6),
    )(
        *(
            pinned(x)
            for x in (
                block_list, land_sea, ice, depth, cur_x, cur_y, wind, wind_rate, dissipation,
                jnp.asarray(component_table()), action, mix1, mix2,
            )
        ),
    )
    return pl.pallas_call(
        last_kernel,
        out_shape=jax.ShapeDtypeStruct(action.shape, F32),
        in_specs=[pl.BlockSpec(memory_space=pltpu.VMEM)] * 6,
        out_specs=hbm,
        scratch_shapes=[
            pltpu.VMEM((K, 256), F32),
            pltpu.VMEM((K // 9, 256), F32),
            dma((9,)), dma((9,)),
        ],
        compiler_params=pltpu.CompilerParams(vmem_limit_bytes=8 * 1024 * 1024),
    )(*state)


def solution(mesh):
    col = P(None, ("band", "grp"))
    flat = P(("band", "grp"))
    grid = P("band", "grp")
    return jax.shard_map(
        on_device,
        mesh=mesh,
        in_specs=(col, flat, grid, grid, grid, grid, grid, grid, P(), P(), P(), P()),
        out_specs=col,
        check_vma=False,
    )
```
